512 devices in a mesh: scene: 8 (over y, core), brick: 64 (over x, z).
Axes of the slice: x: 4, y: 4, z: 16, core: 2. Of those that a mesh axis runs over, the one named last changes fastest.
Arguments:
- tokens: bfloat16 [524288, 384], P(('scene', 'brick')), parts along dimension 0, may hold values from -6 to 6
- token_voxel: int32 [524288], P(('scene', 'brick')), parts along dimension 0, may hold values from 0 to 32767, as said below
- in_weight: bfloat16 [384, 128], replicated, may hold values from -0.3125 to 0.3125
- conv_weight: bfloat16 [27, 128, 128], replicated, may hold values from -0.109375 to 0.109375
- channel_gain: float32 [128], replicated, may hold values from 0.5 to 1.5
- rule_in: int32 [512, 27, 512], P(('scene', 'brick')), parts along dimension 0, may hold values from 0 to 511
- rule_out: int32 [512, 27, 512], P(('scene', 'brick')), parts along dimension 0, may hold values from 0 to 640, as said below
- halo_slots: int32 [512, 2, 64], P(('scene', 'brick')), parts along dimension 0, may hold values from 0 to 511
Outputs:
- voxel_out: bfloat16 [262144, 128], P(('scene', 'brick')), parts along dimension 0
The draws below stay inside these ranges and needn't reach their ends.
There are 8 independent parts, one for each index of `scene`. The reference program is written for one: setup_inputs(seed, part) draws one part's arguments, and reference() takes and returns one part's arrays. A program takes and returns all parts, laid end to end along the dimension named above; an argument that names none is the same for every part. Nothing has to cross between parts.
Inputs may be any that keep to these rules, and one draw needn't show every extreme that they name: `token_voxel`: voxel v belongs to owner v // 512 at slot v % 512. Of one device's tokens at most 32 go to one owner, and on every device some owner gets exactly 32. `rule_out`: below 512: an own voxel slot. 512 + e: row e of the partial outputs for the lower neighbour; 576 + e: row e for the upper neighbour; 640: a padding pair. The first device names no lower rows, the last no upper ones. halo_slots[j, 0, e] receives row e of the lower neighbour's upper partial outputs, halo_slots[j, 1, e] row e of the upper neighbour's lower ones.
All inputs are finite; a program needn't handle non-finite values.
Results may differ from the reference program's by a relative error of at most 0.0052.
Values may be sent and summed in bfloat16 or wider, within the bound.
No kernel may reach another device: no remote copies, remote signals or barrier semaphores. Data moves between devices by JAX's collectives and lax.ppermute only.
A program may use at most 64 MiB of HBM per device.

```python
import jax
import jax.numpy as jnp
from jax import lax

C = 128
TC = 384
OFFS = 27
VOX_DEV = 512
TOK_DEV = 1024
BRICKS = 64
CAP = 32
EDGE = 64
PAIRS = 512
TOKENS = 65536
VOXELS = 32768


def draw_token_voxel(key, part):

    def one_source(source_key):
        keys = jax.random.split(source_key, 5)
        slot_total = BRICKS * CAP
        shuffle = jax.random.permutation(keys[0], slot_total).astype(jnp.int32)
        dest_of_slot = jnp.arange(slot_total, dtype=jnp.int32) // CAP
        priority = jax.random.randint(keys[1], (BRICKS,), 0, 4)
        filled = jax.random.randint(keys[2], (), 0, BRICKS)
        scores = (shuffle + priority[dest_of_slot] * (slot_total // 4)) * slot_total + shuffle
        scores = jnp.where(dest_of_slot == filled, shuffle - slot_total, scores)
        chosen = jnp.argsort(scores, stable=True)[:TOK_DEV].astype(jnp.int32)
        placed = jax.random.permutation(keys[3], chosen)
        owner_dev = placed // CAP
        local_slot = jax.random.randint(keys[4], (TOK_DEV,), 0, VOX_DEV)
        return owner_dev * VOX_DEV + local_slot
    source_keys = jax.random.split(key, BRICKS)
    return jax.vmap(one_source)(source_keys).reshape(-1).astype(jnp.int32)


def draw_rule_out(key, part):
    keys = jax.random.split(key, 4)
    shape = (BRICKS, OFFS, PAIRS)
    live_count = jax.random.randint(keys[0], (BRICKS, OFFS, 1), PAIRS // 2, PAIRS)
    position = jnp.arange(PAIRS, dtype=jnp.int32)[None, None, :]
    kind_code = jax.random.randint(keys[1], shape, 0, 16)
    local_slot = jax.random.randint(keys[2], shape, 0, VOX_DEV)
    edge_row = jax.random.randint(keys[3], shape, 0, EDGE)
    device = jnp.arange(BRICKS, dtype=jnp.int32)[:, None, None]
    dump_row = VOX_DEV + 2 * EDGE
    target = jnp.where(kind_code == 0, VOX_DEV + edge_row, jnp.where(kind_code == 1, VOX_DEV + EDGE + edge_row, local_slot))
    target = jnp.where((kind_code == 0) & (device == 0), dump_row, target)
    target = jnp.where((kind_code == 1) & (device == BRICKS - 1), dump_row, target)
    target = jnp.where(position >= live_count, dump_row, target)
    return target.astype(jnp.int32)


def touch_ends(entries, own_key, low, top_value):
    extent = entries.shape
    index_at = [jax.random.randint(jax.random.fold_in(own_key, axis), (), 0, extent[axis]) for axis in range(len(extent))]
    entries = entries.at[tuple(index_at)].set(low)
    longest = extent.index(max(extent))
    index_at[longest] = (index_at[longest] + 1) % extent[longest]
    return entries.at[tuple(index_at)].set(top_value)


def level_of(stream_key, dims, cuts, low, high):
    def one(dim, shards_of):
        draws = jax.random.uniform(jax.random.fold_in(jax.random.fold_in(stream_key, 6), dim), (shards_of,), jnp.float32, low / len(cuts), high / len(cuts))
        return jnp.repeat(jnp.exp(draws), dims[dim] // shards_of).reshape((-1,) + (1,) * (len(dims) - dim - 1))

    level = one(*cuts[0])
    for cut in cuts[1:]:
        level = level * one(*cut)
    return level


def normal_values(key, dims, scale, limit, pieces=(), kind=jnp.bfloat16):
    factor_of = level_of(key, dims, pieces, -0.22, 0.18) if pieces else 1.0
    values = jax.random.normal(key, dims, jnp.float32) * scale * factor_of
    return jnp.minimum(jnp.maximum(values, -limit), limit).astype(kind)


def setup_inputs(seed: int = 0, part: int = 0) -> dict:
    splits = jax.random.split(jax.random.key(seed), 9)
    own_keys = jax.random.split(jax.random.fold_in(splits[8], part), 9)
    return {
        "tokens": normal_values(own_keys[0], (TOKENS, TC), 1.0, 6.0, ((0, 64),)),
        "token_voxel": draw_token_voxel(jax.random.fold_in(jax.random.fold_in(splits[8], part), 71), part),
        "in_weight": normal_values(splits[2], (TC, C), TC ** -0.5, 0.3125),
        "conv_weight": normal_values(splits[3], (OFFS, C, C), (OFFS * C) ** -0.5, 0.109375),
        "channel_gain": jnp.clip(jax.random.uniform(splits[4], (C,), jnp.float32, 0.5, 1.5), 0.5, 1.5),
        "rule_in": touch_ends(jax.random.randint(own_keys[5], (BRICKS, OFFS, PAIRS), 0, VOX_DEV), jax.random.fold_in(own_keys[5], 1), 0, VOX_DEV - 1).astype(jnp.int32),
        "rule_out": draw_rule_out(jax.random.fold_in(jax.random.fold_in(splits[8], part), 71), part),
        "halo_slots": touch_ends(jax.random.randint(own_keys[7], (BRICKS, 2, EDGE), 0, VOX_DEV), jax.random.fold_in(own_keys[7], 1), 0, VOX_DEV - 1).astype(jnp.int32),
    }


def reference(tokens, token_voxel, in_weight, conv_weight, channel_gain, rule_in, rule_out, halo_slots):
    projected = jnp.dot(tokens, in_weight, preferred_element_type=jnp.float32).astype(jnp.bfloat16)
    voxel_sums = jax.ops.segment_sum(projected.astype(jnp.float32), token_voxel, num_segments=VOXELS)
    counts = jax.ops.segment_sum(jnp.ones(token_voxel.shape, jnp.float32), token_voxel, num_segments=VOXELS)
    voxels = (voxel_sums / jnp.maximum(counts, 1.0)[:, None]).astype(jnp.bfloat16)
    device = jnp.arange(BRICKS, dtype=jnp.int32)[:, None, None]
    lower_dev = jnp.maximum(device - 1, 0)
    upper_dev = jnp.minimum(device + 1, BRICKS - 1)
    low_index = jnp.clip(rule_out - VOX_DEV, 0, EDGE - 1).astype(jnp.int32)
    high_index = jnp.clip(rule_out - VOX_DEV - EDGE, 0, EDGE - 1).astype(jnp.int32)
    lower_target = lower_dev * VOX_DEV + halo_slots[lower_dev, 1, low_index]
    upper_target = upper_dev * VOX_DEV + halo_slots[upper_dev, 0, high_index]
    dump_row = VOX_DEV + 2 * EDGE
    target = jnp.where(rule_out < VOX_DEV, device * VOX_DEV + rule_out, jnp.where(rule_out < VOX_DEV + EDGE, lower_target, jnp.where(rule_out < dump_row, upper_target, VOXELS)))
    lower_off = (rule_out >= VOX_DEV) & (rule_out < VOX_DEV + EDGE) & (device == 0)
    upper_off = (rule_out >= VOX_DEV + EDGE) & (rule_out < dump_row) & (device == BRICKS - 1)
    target = jnp.where(lower_off | upper_off, VOXELS, target).astype(jnp.int32)
    source = (device * VOX_DEV + rule_in).astype(jnp.int32)

    def offset_step(totals, offset_items):
        weight, source_k, target_k = offset_items
        gathered = jnp.take(voxels, source_k.reshape(-1), axis=0)
        products = jnp.dot(gathered, weight, preferred_element_type=jnp.float32)
        return (totals.at[target_k.reshape(-1)].add(products), None)
    start = jnp.zeros((VOXELS + 1, C), jnp.float32)
    totals = lax.scan(offset_step, start, (conv_weight, jnp.transpose(source, (1, 0, 2)), jnp.transpose(target, (1, 0, 2))))[0]
    conv_sum = totals[:VOXELS]
    inv_rms = lax.rsqrt(lax.optimization_barrier(jnp.mean(conv_sum * conv_sum, axis=1, keepdims=True)) + 1e-05)
    return (voxels.astype(jnp.float32) + jax.nn.relu(conv_sum * inv_rms * channel_gain)).astype(jnp.bfloat16)
```

```python
import functools

import jax
import jax.numpy as jnp
import numpy as np
from jax import lax
from jax.experimental import pallas as pl
from jax.experimental.pallas import tpu as pltpu
from jax.sharding import PartitionSpec as P

VOX = 512
LANES = 128
BF = jnp.bfloat16
F32 = jnp.float32
VMEM_LIMIT = 50 * 1024 * 1024


def passed_along(block, axis, distance):
    devices = range(lax.axis_size(axis))
    route = [(i - distance, i) for i in devices if i - distance in devices]
    return lax.ppermute(block, axis, route)


def dot(a, b):
    return jnp.dot(a, b, preferred_element_type=F32)


def dot_t(a, b):
    return lax.dot_general(a, b, (((1,), (1,)), ((), ())), preferred_element_type=F32)


def row_iota(rows):
    return lax.broadcasted_iota(jnp.int32, (rows, LANES), 0).astype(F32).astype(BF)


def one_hot_rows(numbers, value, start):
    rows = numbers.shape[0]
    here = jnp.clip(value - start, -1, rows).astype(F32).astype(BF)
    return jnp.where(
        numbers == jnp.broadcast_to(here, numbers.shape), jnp.ones_like(numbers), jnp.zeros_like(numbers)
    )


def prep_kernel(bricks, cap, me_ref, voxel_ref, tokens_ref, weight_ref, extra_ref, out_ref):
    per = cap + 2
    rows = bricks * per
    chunks = voxel_ref.shape[0]
    projected = dot(tokens_ref[...], weight_ref[...]).astype(BF)
    t_from = lax.broadcasted_iota(jnp.int32, (LANES, LANES), 0)
    t_to = lax.broadcasted_iota(jnp.int32, (LANES, LANES), 1)
    upper = jnp.where(t_from <= t_to, 1.0, 0.0).astype(BF)
    brick_id = lax.broadcasted_iota(jnp.int32, (bricks, LANES), 0)
    owners = [voxel_ref[b : b + 1, :] // VOX for b in range(chunks)]
    slots = [voxel_ref[b : b + 1, :] % VOX for b in range(chunks)]
    member = [jnp.where(brick_id == o, 1.0, 0.0) for o in owners]
    running = dot(jnp.concatenate(member, axis=0).astype(BF), upper)
    before = jnp.zeros((bricks, 1), F32)
    shift = me_ref[0] * per
    lane_id = lax.broadcasted_iota(jnp.int32, (LANES, LANES), 0)
    position, slot_cols = [], []
    for b in range(chunks):
        run = running[b * bricks : (b + 1) * bricks]
        rank = jnp.sum(member[b] * (run + before), axis=0, keepdims=True).astype(jnp.int32) - 1
        before = before + run[:, LANES - 1 :]
        position.append(owners[b] * per + rank)
        at = lane_id == (rank + shift) % LANES
        plus = slots[b] + 1
        low = jnp.where(at, (plus % 256).astype(F32), 0.0)
        high = jnp.where(at, (plus // 256).astype(F32), 0.0)
        slot_cols.append(jnp.concatenate([low, high], axis=0).astype(BF))
    slot_rows = dot_t(
        jnp.concatenate(member, axis=1).astype(BF), jnp.concatenate(slot_cols, axis=1)
    ).astype(BF)
    source = jnp.concatenate([projected, slot_rows[:, :LANES], slot_rows[:, LANES:]], axis=0)
    position.append(extra_ref[...])
    size = 256
    for start in range(0, rows, size):
        n = min(size, rows - start)
        numbers = row_iota(n)
        table = jnp.concatenate([one_hot_rows(numbers, p, start) for p in position], axis=1)
        out_ref[start : start + n, :] = dot(table, source).astype(BF)


def rules_kernel(rule_in_ref, rule_out_ref, own_ref, edge_ref):
    k = pl.program_id(0)
    pairs = rule_in_ref.shape[1]
    source = rule_in_ref[pl.ds(k, 1), :]
    target = rule_out_ref[pl.ds(k, 1), :]
    numbers = row_iota(256)

    def table(value, start, n):
        return jnp.concatenate(
            [
                one_hot_rows(numbers[:n], value[:, c : c + LANES], start)
                for c in range(0, pairs, LANES)
            ],
            axis=1,
        )

    pick = jnp.concatenate([table(source, s, 256) for s in range(0, VOX, 256)], axis=0)
    for s in range(0, VOX, 256):
        own_ref[0, s : s + 256, :] = dot_t(table(target, s, 256), pick).astype(BF)
    edge_ref[0] = dot_t(table(target, VOX, edge_ref.shape[1]), pick).astype(BF)


def mix(counts, voxels, weights):
    width = voxels.shape[1]
    offsets = weights.shape[0] // width
    rows = counts.shape[0] // offsets
    gathered = dot(counts, voxels).astype(BF)
    side = jnp.concatenate([gathered[k * rows : (k + 1) * rows] for k in range(offsets)], axis=1)
    return dot(side, weights)


def voxel_kernel(bricks, cap, arrived_ref, class_ref, edge_counts_ref, conv_ref, voxels_ref, lower_ref, upper_ref):
    per = cap + 2
    chunks = class_ref.shape[0]
    arrived = arrived_ref[...]
    numbers = row_iota(256)
    pick = jnp.concatenate(
        [one_hot_rows(numbers[: 2 * bricks], class_ref[c : c + 1, :], 0) for c in range(chunks)], axis=1
    )
    coded = dot(pick, arrived)
    low, high = coded[:bricks], coded[bricks:]
    begin = lax.broadcasted_iota(jnp.int32, (bricks, LANES), 0) * per
    lane = lax.broadcasted_iota(jnp.int32, (bricks, LANES), 1)
    stays = lane >= begin % LANES
    spread = jnp.concatenate(
        [
            jnp.concatenate([jnp.where(stays, x, 0.0), jnp.where(stays, 0.0, x)], axis=0)
            for x in (low, high)
        ],
        axis=1,
    ).astype(BF)
    chunk_id = lax.broadcasted_iota(jnp.int32, (32, 2 * bricks), 0)
    column = lax.broadcasted_iota(jnp.int32, (32, 2 * bricks), 1)
    wraps = jnp.where(column >= bricks, 1, 0)
    chunk_of = ((column - wraps * bricks) * per) // LANES + wraps
    lined = dot(jnp.where(chunk_id == chunk_of, 1.0, 0.0).astype(BF), spread)
    slot = (lined[:, :LANES] + 256.0 * lined[:, LANES:]).astype(jnp.int32) - 1
    right = jnp.concatenate([arrived, jnp.ones_like(arrived)], axis=1)
    parts = []
    for s in range(0, VOX, 256):
        table = jnp.concatenate(
            [one_hot_rows(numbers, slot[c : c + 1, :], s) for c in range(chunks)], axis=1
        )
        both = dot(table, right)
        parts.append((both[:, :LANES] / jnp.maximum(both[:, LANES:], 1.0)).astype(BF))
    voxels = jnp.concatenate(parts, axis=0)
    voxels_ref[...] = voxels
    edge = mix(edge_counts_ref[...], voxels, conv_ref[...]).astype(BF)
    half = lower_ref.shape[0]
    lower_ref[...] = edge[:half]
    upper_ref[...] = edge[half:]


def own_kernel(counts_ref, voxels_ref, conv_ref, out_ref):
    @pl.when(pl.program_id(0) == 0)
    def _():
        out_ref[...] = jnp.zeros_like(out_ref)

    out_ref[...] += mix(counts_ref[...], voxels_ref[...], conv_ref[...])


def final_kernel(own_ref, voxels_ref, halo_ref, from_lower_ref, from_upper_ref, gain_ref, out_ref):
    numbers = row_iota(256)
    partial = jnp.concatenate([from_lower_ref[...], from_upper_ref[...]], axis=0)
    for s in range(0, VOX, 256):
        place = one_hot_rows(numbers, halo_ref[...], s)
        conv_sum = own_ref[s : s + 256, :] + dot(place, partial)
        inv_rms = lax.rsqrt(jnp.mean(conv_sum * conv_sum, axis=1, keepdims=True) + 1e-05)
        fresh = jnp.maximum(conv_sum * inv_rms * gain_ref[...], 0.0)
        out_ref[s : s + 256, :] = (voxels_ref[s : s + 256, :].astype(F32) + fresh).astype(BF)


def params(semantics=None):
    return pltpu.CompilerParams(vmem_limit_bytes=VMEM_LIMIT, dimension_semantics=semantics)


def cost(flops, moved):
    return pl.CostEstimate(flops=int(flops), bytes_accessed=int(moved), transcendentals=0)


def per_device(
    tokens, token_voxel, in_weight, conv_weight, channel_gain, rule_in, rule_out, halo_slots
):
    bricks = lax.axis_size("brick")
    tok_count = tokens.shape[0]
    cap = 2 * tok_count // bricks
    per = cap + 2
    rows = bricks * per
    offsets, width = conv_weight.shape[0], conv_weight.shape[2]
    pairs = rule_in.shape[2]
    edges = 2 * halo_slots.shape[2]
    me = lax.axis_index("brick").astype(jnp.int32).reshape(1)
    row_number = np.arange(rows)
    brick_of, rank_of = row_number // per, row_number % per
    classes = np.where(rank_of >= cap, (rank_of - cap) * bricks + brick_of, -1)
    classes = jnp.asarray(classes.reshape(rows // LANES, LANES), jnp.int32)
    extra = np.concatenate([np.arange(bricks) * per + cap, np.arange(bricks) * per + cap + 1])
    extra = jnp.asarray(extra.reshape(1, 2 * bricks), jnp.int32)
    conv_rows = conv_weight.reshape(offsets * width, width)
    vmem = pl.BlockSpec(memory_space=pltpu.VMEM)

    send = pl.pallas_call(
        functools.partial(prep_kernel, bricks, cap),
        out_shape=jax.ShapeDtypeStruct((rows, width), BF),
        in_specs=[pl.BlockSpec(memory_space=pltpu.SMEM)] + [vmem] * 4,
        out_specs=vmem,
        compiler_params=params(),
        cost_estimate=cost(2 * rows * 1152 * width, 2_000_000),
        name="prep",
    )(me, token_voxel.reshape(tok_count // LANES, LANES), tokens, in_weight, extra)

    arrived = lax.all_to_all(
        send.reshape(bricks, per // 2, 2, width), "brick", split_axis=0, concat_axis=0, tiled=True
    ).reshape(rows, width)

    own_counts, edge_counts = pl.pallas_call(
        rules_kernel,
        out_shape=(
            jax.ShapeDtypeStruct((offsets, VOX, VOX), BF),
            jax.ShapeDtypeStruct((offsets, edges, VOX), BF),
        ),
        grid=(offsets,),
        in_specs=[pl.BlockSpec((offsets, pairs), lambda k: (0, 0))] * 2,
        out_specs=(
            pl.BlockSpec((1, VOX, VOX), lambda k: (k, 0, 0)),
            pl.BlockSpec((1, edges, VOX), lambda k: (k, 0, 0)),
        ),
        compiler_params=params(("arbitrary",)),
        cost_estimate=cost(2 * offsets * (VOX + edges) * VOX * pairs, 2 * offsets * (VOX + edges) * VOX),
        name="rules",
    )(rule_in[0], rule_out[0])

    voxels, to_lower, to_upper = pl.pallas_call(
        functools.partial(voxel_kernel, bricks, cap),
        out_shape=(
            jax.ShapeDtypeStruct((VOX, width), BF),
            jax.ShapeDtypeStruct((edges // 2, width), BF),
            jax.ShapeDtypeStruct((edges // 2, width), BF),
        ),
        in_specs=[vmem] * 4,
        out_specs=(vmem, vmem, vmem),
        compiler_params=params(),
        cost_estimate=cost(2 * offsets * edges * VOX * width, 6_000_000),
        name="voxel",
    )(arrived, classes, edge_counts.reshape(offsets * edges, VOX), conv_rows)

    from_lower = passed_along(to_upper, "brick", 1)
    from_upper = passed_along(to_lower, "brick", -1)

    group = 3
    own = pl.pallas_call(
        own_kernel,
        out_shape=jax.ShapeDtypeStruct((VOX, width), F32),
        grid=(offsets // group,),
        in_specs=[
            pl.BlockSpec((group * VOX, VOX), lambda k: (k, 0)),
            pl.BlockSpec((VOX, width), lambda k: (0, 0)),
            pl.BlockSpec((group * width, width), lambda k: (k, 0)),
        ],
        out_specs=pl.BlockSpec((VOX, width), lambda k: (0, 0)),
        compiler_params=params(("arbitrary",)),
        cost_estimate=cost(2 * offsets * VOX * (VOX + width) * width, 2 * offsets * VOX * VOX),
        name="own",
    )(own_counts.reshape(offsets * VOX, VOX), voxels, conv_rows)

    return pl.pallas_call(
        final_kernel,
        out_shape=jax.ShapeDtypeStruct((VOX, width), BF),
        in_specs=[vmem] * 6,
        out_specs=vmem,
        compiler_params=params(),
        cost_estimate=cost(2 * VOX * width * width, 1_000_000),
        name="final",
    )(own, voxels, halo_slots.reshape(1, edges), from_lower, from_upper, channel_gain.reshape(1, width))


def solution(mesh):
    return jax.shard_map(
        per_device,
        mesh=mesh,
        in_specs=(
            P(("scene", "brick"), None),
            P(("scene", "brick")),
            P(),
            P(),
            P(),
            P(("scene", "brick"), None, None),
            P(("scene", "brick"), None, None),
            P(("scene", "brick"), None, None),
        ),
        out_specs=P(("scene", "brick"), None),
        check_vma=False,
    )
```

```python
import functools

import jax
import jax.numpy as jnp
import numpy as np
from jax import lax
from jax.experimental import pallas as pl
from jax.experimental.pallas import tpu as pltpu
from jax.sharding import PartitionSpec as P

VOX = 512
LANES = 128
BF = jnp.bfloat16
F32 = jnp.float32
PREP_MIB, RULES_MIB, VOXEL_MIB, OWN_MIB, FINAL_MIB = 16, 8, 16, 20, 4
NEAR, FAR_PARTS, PACK = 12, 5, 256


def exchanged(block, axis, first):
    pairs = [(i, i + 1) for i in range(first, lax.axis_size(axis) - 1, 2)]
    return lax.ppermute(block, axis, pairs + [(b, a) for a, b in pairs])


def dot(a, b):
    return jnp.dot(a, b, preferred_element_type=F32)


def dot_t(a, b):
    return lax.dot_general(a, b, (((1,), (1,)), ((), ())), preferred_element_type=F32)


def row_iota(rows):
    return lax.broadcasted_iota(jnp.int32, (rows, LANES), 0).astype(F32).astype(BF)


def one_hot_rows(numbers, value, start):
    rows = numbers.shape[0]
    here = jnp.clip(value - start, -1, rows).astype(F32).astype(BF)
    return jnp.where(
        numbers == jnp.broadcast_to(here, numbers.shape), jnp.ones_like(numbers), jnp.zeros_like(numbers)
    )


def prep_kernel(
    bricks, cap, me_ref, voxel_hbm, tokens_hbm, weight_hbm, out_hbm, voxel_ref, tokens_ref, weight_ref, out_ref, sems, out_sems
):
    copies = [
        pltpu.make_async_copy(src, dst, sems.at[i])
        for i, (src, dst) in enumerate(
            [(voxel_hbm, voxel_ref), (weight_hbm, weight_ref), (tokens_hbm, tokens_ref)]
        )
    ]
    for copy in copies:
        copy.start()
    copies[0].wait()
    per = cap + 2
    rows = bricks * per
    chunks = voxel_ref.shape[0]
    t_from = lax.broadcasted_iota(jnp.int32, (LANES, LANES), 0)
    t_to = lax.broadcasted_iota(jnp.int32, (LANES, LANES), 1)
    upper = jnp.where(t_from <= t_to, 1.0, 0.0).astype(BF)
    brick_id = lax.broadcasted_iota(jnp.int32, (bricks, LANES), 0)
    owners = [voxel_ref[b : b + 1, :] // VOX for b in range(chunks)]
    slots = [voxel_ref[b : b + 1, :] % VOX for b in range(chunks)]
    member = [jnp.where(brick_id == o, 1.0, 0.0) for o in owners]
    running = dot(jnp.concatenate(member, axis=0).astype(BF), upper)
    before = jnp.zeros((bricks, 1), F32)
    shift = me_ref[0] * per
    lane_id = lax.broadcasted_iota(jnp.int32, (LANES, LANES), 0)
    position, slot_cols = [], []
    for b in range(chunks):
        run = running[b * bricks : (b + 1) * bricks]
        rank = jnp.sum(member[b] * (run + before), axis=0, keepdims=True).astype(jnp.int32) - 1
        before = before + run[:, LANES - 1 :]
        position.append(owners[b] * per + rank)
        at = lane_id == (rank + shift) % LANES
        plus = slots[b] + 1
        low = jnp.where(at, (plus % 256).astype(F32), 0.0)
        high = jnp.where(at, (plus // 256).astype(F32), 0.0)
        slot_cols.append(jnp.concatenate([low, high], axis=0).astype(BF))
    slot_rows = dot_t(
        jnp.concatenate(member, axis=1).astype(BF), jnp.concatenate(slot_cols, axis=1)
    ).astype(BF)
    column = lax.broadcasted_iota(jnp.int32, (1, LANES), 1)
    position.append(jnp.where(column < bricks, column * per + cap, (column - bricks) * per + cap + 1))
    copies[1].wait()
    copies[2].wait()
    projected = dot(tokens_ref[...], weight_ref[...]).astype(BF)
    source = jnp.concatenate([projected, slot_rows[:, :LANES], slot_rows[:, LANES:]], axis=0)
    sends = []
    for i, start in enumerate(range(0, rows, PACK)):
        n = min(PACK, rows - start)
        numbers = row_iota(n)
        table = jnp.concatenate([one_hot_rows(numbers, p, start) for p in position], axis=1)
        out_ref[start : start + n, :] = dot(table, source).astype(BF)
        part = pl.ds(start, n)
        sends.append(pltpu.make_async_copy(out_ref.at[part], out_hbm.at[part], out_sems.at[i]))
        sends[i].start()
    for send in sends:
        send.wait()


def rules_kernel(rule_in_ref, rule_out_ref, own_ref, edge_ref):
    k = pl.program_id(0)
    pairs = rule_in_ref.shape[1]
    source = rule_in_ref[pl.ds(k, 1), :]
    target = rule_out_ref[pl.ds(k, 1), :]
    numbers = row_iota(256)

    def table(value, start, n):
        return jnp.concatenate(
            [
                one_hot_rows(numbers[:n], value[:, c : c + LANES], start)
                for c in range(0, pairs, LANES)
            ],
            axis=1,
        )

    pick = jnp.concatenate([table(source, s, 256) for s in range(0, VOX, 256)], axis=0)
    place = jnp.concatenate([table(target, s, 256) for s in range(0, VOX, 256)], axis=0)
    own_ref[0] = dot_t(pick, place).astype(BF)
    edge_ref[0] = dot_t(table(target, VOX, edge_ref.shape[1]), pick).astype(BF)


def mix(counts, voxels, weights):
    width = voxels.shape[1]
    offsets = weights.shape[0] // width
    rows = counts.shape[0] // offsets
    gathered = dot(counts, voxels).astype(BF)
    side = jnp.concatenate([gathered[k * rows : (k + 1) * rows] for k in range(offsets)], axis=1)
    return dot(side, weights)


def voxel_kernel(
    bricks, cap, me_ref, arrived_ref, class_ref, edge_hbm, conv_hbm, own_hbm,
    voxels_ref, first_ref, second_ref, conv_ref, near_ref, edge_counts_ref, sems,
):
    near = near_ref.shape[0]
    copies = [
        pltpu.make_async_copy(src, dst, sems.at[i])
        for i, (src, dst) in enumerate(
            [(edge_hbm, edge_counts_ref), (conv_hbm, conv_ref), (own_hbm.at[pl.ds(0, near)], near_ref)]
        )
    ]
    for copy in copies:
        copy.start()
    per = cap + 2
    chunks = class_ref.shape[0]
    arrived = arrived_ref[...]
    numbers = row_iota(256)
    pick = jnp.concatenate(
        [one_hot_rows(numbers[: 2 * bricks], class_ref[c : c + 1, :], 0) for c in range(chunks)], axis=1
    )
    coded = dot(pick, arrived)
    low, high = coded[:bricks], coded[bricks:]
    begin = lax.broadcasted_iota(jnp.int32, (bricks, LANES), 0) * per
    lane = lax.broadcasted_iota(jnp.int32, (bricks, LANES), 1)
    stays = lane >= begin % LANES
    spread = jnp.concatenate(
        [
            jnp.concatenate([jnp.where(stays, x, 0.0), jnp.where(stays, 0.0, x)], axis=0)
            for x in (low, high)
        ],
        axis=1,
    ).astype(BF)
    chunk_id = lax.broadcasted_iota(jnp.int32, (32, 2 * bricks), 0)
    column = lax.broadcasted_iota(jnp.int32, (32, 2 * bricks), 1)
    wraps = jnp.where(column >= bricks, 1, 0)
    chunk_of = ((column - wraps * bricks) * per) // LANES + wraps
    lined = dot(jnp.where(chunk_id == chunk_of, 1.0, 0.0).astype(BF), spread)
    slot = (lined[:, :LANES] + 256.0 * lined[:, LANES:]).astype(jnp.int32) - 1
    right = jnp.concatenate([arrived, jnp.ones_like(arrived)], axis=1)
    parts = []
    for s in range(0, VOX, 256):
        table = jnp.concatenate(
            [one_hot_rows(numbers, slot[c : c + 1, :], s) for c in range(chunks)], axis=1
        )
        both = dot(table, right)
        parts.append((both[:, :LANES] / jnp.maximum(both[:, LANES:], 1.0)).astype(BF))
    voxels = jnp.concatenate(parts, axis=0)
    voxels_ref[...] = voxels
    copies[0].wait()
    copies[1].wait()
    edge = mix(edge_counts_ref[...], voxels, conv_ref[...]).astype(BF)
    half = first_ref.shape[0]
    odd = me_ref[0] % 2 == 1
    first_ref[...] = jnp.where(odd, edge[:half], edge[half:])
    second_ref[...] = jnp.where(odd, edge[half:], edge[:half])
    copies[2].wait()


def own_kernel(near_ref, own_hbm, voxels_ref, conv_ref, out_ref, far_ref, sems):
    near, far = near_ref.shape[0], far_ref.shape[0]
    parts = sems.shape[0]
    size = far // parts
    copies = [
        pltpu.make_async_copy(
            own_hbm.at[pl.ds(near + c * size, size)], far_ref.at[pl.ds(c * size, size)], sems.at[c]
        )
        for c in range(parts)
    ]
    for copy in copies:
        copy.start()
    width = voxels_ref.shape[1]
    starts = range(0, conv_ref.shape[0], width)
    wide = jnp.concatenate([conv_ref[s : s + width, :] for s in starts], axis=1)
    terms = lax.dot_general(
        wide, voxels_ref[...], (((0,), (1,)), ((), ())), preferred_element_type=F32
    ).astype(BF)
    side = jnp.concatenate([terms[s : s + width] for s in starts], axis=1)
    total = dot(side[:, :near], near_ref[...])
    for c in range(parts):
        copies[c].wait()
        begin = c * size
        total += dot(side[:, near + begin : near + begin + size], far_ref[begin : begin + size, :])
    out_ref[...] = total.T


def final_kernel(me_ref, own_ref, voxels_ref, halo_ref, first_ref, second_ref, gain_ref, out_ref):
    numbers = row_iota(256)
    odd = me_ref[0] % 2 == 1
    first, second = first_ref[...], second_ref[...]
    lower, upper = jnp.where(odd, first, second), jnp.where(odd, second, first)
    partial = jnp.concatenate([lower, upper], axis=0)
    for s in range(0, VOX, 256):
        place = one_hot_rows(numbers, halo_ref[...], s)
        conv_sum = own_ref[s : s + 256, :] + dot(place, partial)
        inv_rms = lax.rsqrt(jnp.mean(conv_sum * conv_sum, axis=1, keepdims=True) + 1e-05)
        fresh = jnp.maximum(conv_sum * inv_rms * gain_ref[...], 0.0)
        out_ref[s : s + 256, :] = (voxels_ref[s : s + 256, :].astype(F32) + fresh).astype(BF)


def params(mib, semantics=None):
    return pltpu.CompilerParams(vmem_limit_bytes=mib * 1024 * 1024, dimension_semantics=semantics)


def in_hbm(x):
    return pltpu.with_memory_space_constraint(x, pltpu.HBM)


def cost(flops, moved):
    return pl.CostEstimate(flops=int(flops), bytes_accessed=int(moved), transcendentals=0)


def per_device(
    tokens, token_voxel, in_weight, conv_weight, channel_gain, rule_in, rule_out, halo_slots
):
    bricks = lax.axis_size("brick")
    tok_count = tokens.shape[0]
    cap = 2 * tok_count // bricks
    per = cap + 2
    rows = bricks * per
    offsets, width = conv_weight.shape[0], conv_weight.shape[2]
    pairs = rule_in.shape[2]
    edges = 2 * halo_slots.shape[2]
    me = lax.axis_index("brick").astype(jnp.int32).reshape(1)
    row_number = np.arange(rows)
    brick_of, rank_of = row_number // per, row_number % per
    classes = np.where(rank_of >= cap, (rank_of - cap) * bricks + brick_of, -1)
    classes = jnp.asarray(classes.reshape(rows // LANES, LANES), jnp.int32)
    conv_rows = conv_weight.reshape(offsets * width, width)
    vmem = pl.BlockSpec(memory_space=pltpu.VMEM)
    hbm = pl.BlockSpec(memory_space=pl.ANY)
    smem = pl.BlockSpec(memory_space=pltpu.SMEM)

    send = pl.pallas_call(
        functools.partial(prep_kernel, bricks, cap),
        out_shape=pltpu.HBM((rows, width), BF),
        in_specs=[smem] + [hbm] * 3,
        out_specs=hbm,
        scratch_shapes=[
            pltpu.VMEM((tok_count // LANES, LANES), jnp.int32),
            pltpu.VMEM(tokens.shape, BF),
            pltpu.VMEM(in_weight.shape, BF),
            pltpu.VMEM((rows, width), BF),
            pltpu.SemaphoreType.DMA((3,)),
            pltpu.SemaphoreType.DMA((-(-rows // PACK),)),
        ],
        compiler_params=params(PREP_MIB),
        cost_estimate=cost(2 * rows * 1152 * width, 2_000_000),
        name="prep",
    )(me, *[in_hbm(x) for x in (token_voxel.reshape(tok_count // LANES, LANES), tokens, in_weight)])

    arrived = lax.all_to_all(
        send.reshape(bricks, per // 2, 2, width), "brick", split_axis=0, concat_axis=0, tiled=True
    ).reshape(rows, width)

    own_counts, edge_counts = pl.pallas_call(
        rules_kernel,
        out_shape=(
            pltpu.HBM((offsets, VOX, VOX), BF),
            pltpu.HBM((offsets, edges, VOX), BF),
        ),
        grid=(offsets,),
        in_specs=[pl.BlockSpec((offsets, pairs), lambda k: (0, 0))] * 2,
        out_specs=(
            pl.BlockSpec((1, VOX, VOX), lambda k: (k, 0, 0)),
            pl.BlockSpec((1, edges, VOX), lambda k: (k, 0, 0)),
        ),
        compiler_params=params(RULES_MIB, ("arbitrary",)),
        cost_estimate=cost(2 * offsets * (VOX + edges) * VOX * pairs, 2 * offsets * (VOX + edges) * VOX),
        name="rules",
    )(rule_in[0], rule_out[0])

    own_counts = in_hbm(own_counts.reshape(offsets * VOX, VOX))
    edge_counts = in_hbm(edge_counts.reshape(offsets * edges, VOX))
    near = NEAR * VOX
    voxels, first, second, conv_near, near_counts = pl.pallas_call(
        functools.partial(voxel_kernel, bricks, cap),
        out_shape=(
            jax.ShapeDtypeStruct((VOX, width), BF),
            jax.ShapeDtypeStruct((edges // 2, width), BF),
            jax.ShapeDtypeStruct((edges // 2, width), BF),
            pltpu.VMEM((offsets * width, width), BF),
            pltpu.VMEM((near, VOX), BF),
        ),
        in_specs=[smem] + [vmem] * 2 + [hbm] * 3,
        out_specs=(vmem,) * 5,
        scratch_shapes=[pltpu.VMEM((offsets * edges, VOX), BF), pltpu.SemaphoreType.DMA((3,))],
        compiler_params=params(VOXEL_MIB),
        cost_estimate=cost(2 * offsets * edges * VOX * width, 6_000_000),
        name="voxel",
    )(me, arrived, classes, edge_counts, in_hbm(conv_rows), own_counts)

    from_first = exchanged(first, "brick", 0)
    from_second = exchanged(second, "brick", 1)

    own = pl.pallas_call(
        own_kernel,
        out_shape=jax.ShapeDtypeStruct((VOX, width), F32),
        in_specs=[vmem, hbm, vmem, vmem],
        out_specs=vmem,
        scratch_shapes=[pltpu.VMEM((offsets * VOX - near, VOX), BF), pltpu.SemaphoreType.DMA((FAR_PARTS,))],
        compiler_params=params(OWN_MIB),
        cost_estimate=cost(2 * offsets * VOX * (VOX + width) * width, 2 * offsets * VOX * VOX),
        name="own",
    )(near_counts, own_counts, voxels, conv_near)

    return pl.pallas_call(
        final_kernel,
        out_shape=jax.ShapeDtypeStruct((VOX, width), BF),
        in_specs=[smem] + [vmem] * 6,
        out_specs=vmem,
        compiler_params=params(FINAL_MIB),
        cost_estimate=cost(2 * VOX * width * width, 1_000_000),
        name="final",
    )(me, own, voxels, halo_slots.reshape(1, edges), from_first, from_second, channel_gain.reshape(1, width))


def solution(mesh):
    return jax.shard_map(
        per_device,
        mesh=mesh,
        in_specs=(
            P(("scene", "brick"), None),
            P(("scene", "brick")),
            P(),
            P(),
            P(),
            P(("scene", "brick"), None, None),
            P(("scene", "brick"), None, None),
            P(("scene", "brick"), None, None),
        ),
        out_specs=P(("scene", "brick"), None),
        check_vma=False,
    )
```

```python
import functools

import jax
import jax.numpy as jnp
import numpy as np
from jax import lax
from jax.experimental import pallas as pl
from jax.experimental.pallas import tpu as pltpu
from jax.sharding import PartitionSpec as P

VOX = 512
LANES = 128
BF = jnp.bfloat16
F32 = jnp.float32
PREP_MIB, RULES_MIB, VOXEL_MIB, OWN_MIB, FINAL_MIB = 16, 8, 16, 20, 4
KEEP, NEAR, FAR_PARTS, PACK = 3, 10, 4, 256


def exchanged(block, axis, first):
    pairs = [(i, i + 1) for i in range(first, lax.axis_size(axis) - 1, 2)]
    return lax.ppermute(block, axis, pairs + [(b, a) for a, b in pairs])


def dot(a, b):
    return jnp.dot(a, b, preferred_element_type=F32)


def dot_t(a, b):
    return lax.dot_general(a, b, (((1,), (1,)), ((), ())), preferred_element_type=F32)


def row_iota(rows):
    return lax.broadcasted_iota(jnp.int32, (rows, LANES), 0).astype(F32).astype(BF)


def one_hot_rows(numbers, value, start):
    rows = numbers.shape[0]
    here = jnp.clip(value - start, -1, rows).astype(F32).astype(BF)
    return jnp.where(
        numbers == jnp.broadcast_to(here, numbers.shape), jnp.ones_like(numbers), jnp.zeros_like(numbers)
    )


def prep_kernel(
    bricks, cap, me_ref, voxel_hbm, tokens_hbm, weight_hbm, out_hbm, voxel_ref, tokens_ref, weight_ref, out_ref, sems, out_sems
):
    copies = [
        pltpu.make_async_copy(src, dst, sems.at[i])
        for i, (src, dst) in enumerate(
            [(voxel_hbm, voxel_ref), (weight_hbm, weight_ref), (tokens_hbm, tokens_ref)]
        )
    ]
    for copy in copies:
        copy.start()
    copies[0].wait()
    per = cap + 2
    rows = bricks * per
    chunks = voxel_ref.shape[0]
    t_from = lax.broadcasted_iota(jnp.int32, (LANES, LANES), 0)
    t_to = lax.broadcasted_iota(jnp.int32, (LANES, LANES), 1)
    upper = jnp.where(t_from <= t_to, 1.0, 0.0).astype(BF)
    brick_id = lax.broadcasted_iota(jnp.int32, (bricks, LANES), 0)
    owners = [voxel_ref[b : b + 1, :] // VOX for b in range(chunks)]
    slots = [voxel_ref[b : b + 1, :] % VOX for b in range(chunks)]
    member = [jnp.where(brick_id == o, 1.0, 0.0) for o in owners]
    running = dot(jnp.concatenate(member, axis=0).astype(BF), upper)
    before = jnp.zeros((bricks, 1), F32)
    shift = me_ref[0] * per
    lane_id = lax.broadcasted_iota(jnp.int32, (LANES, LANES), 0)
    position, slot_cols = [], []
    for b in range(chunks):
        run = running[b * bricks : (b + 1) * bricks]
        rank = jnp.sum(member[b] * (run + before), axis=0, keepdims=True).astype(jnp.int32) - 1
        before = before + run[:, LANES - 1 :]
        position.append(owners[b] * per + rank)
        at = lane_id == (rank + shift) % LANES
        plus = slots[b] + 1
        low = jnp.where(at, (plus % 256).astype(F32), 0.0)
        high = jnp.where(at, (plus // 256).astype(F32), 0.0)
        slot_cols.append(jnp.concatenate([low, high], axis=0).astype(BF))
    slot_rows = dot_t(
        jnp.concatenate(member, axis=1).astype(BF), jnp.concatenate(slot_cols, axis=1)
    ).astype(BF)
    column = lax.broadcasted_iota(jnp.int32, (1, LANES), 1)
    position.append(jnp.where(column < bricks, column * per + cap, (column - bricks) * per + cap + 1))
    copies[1].wait()
    copies[2].wait()
    projected = dot(tokens_ref[...], weight_ref[...]).astype(BF)
    source = jnp.concatenate([projected, slot_rows[:, :LANES], slot_rows[:, LANES:]], axis=0)
    sends = []
    for i, start in enumerate(range(0, rows, PACK)):
        n = min(PACK, rows - start)
        numbers = row_iota(n)
        table = jnp.concatenate([one_hot_rows(numbers, p, start) for p in position], axis=1)
        out_ref[start : start + n, :] = dot(table, source).astype(BF)
        part = pl.ds(start, n)
        sends.append(pltpu.make_async_copy(out_ref.at[part], out_hbm.at[part], out_sems.at[i]))
        sends[i].start()
    for send in sends:
        send.wait()


def rules_kernel(rule_in_ref, rule_out_ref, keep_ref, own_ref, edge_ref):
    k = pl.program_id(0)
    pairs = rule_in_ref.shape[1]
    source = rule_in_ref[pl.ds(k, 1), :]
    target = rule_out_ref[pl.ds(k, 1), :]
    numbers = row_iota(256)

    def table(value, start, n):
        return jnp.concatenate(
            [
                one_hot_rows(numbers[:n], value[:, c : c + LANES], start)
                for c in range(0, pairs, LANES)
            ],
            axis=1,
        )

    pick = jnp.concatenate([table(source, s, 256) for s in range(0, VOX, 256)], axis=0)
    place = jnp.concatenate([table(target, s, 256) for s in range(0, VOX, 256)], axis=0)
    counts = dot_t(pick, place).astype(BF)

    @pl.when(k < KEEP)
    def _():
        keep_ref[0] = counts

    @pl.when(k >= KEEP)
    def _():
        own_ref[0] = counts

    edge_ref[0] = dot_t(table(target, VOX, edge_ref.shape[1]), pick).astype(BF)


def mix(counts, voxels, weights):
    width = voxels.shape[1]
    offsets = weights.shape[0] // width
    rows = counts.shape[0] // offsets
    gathered = dot(counts, voxels).astype(BF)
    side = jnp.concatenate([gathered[k * rows : (k + 1) * rows] for k in range(offsets)], axis=1)
    return dot(side, weights)


def voxel_kernel(
    bricks, cap, me_ref, arrived_ref, class_ref, conv_ref, edge_hbm, own_hbm,
    voxels_ref, first_ref, second_ref, near_ref, edge_counts_ref, sems,
):
    near = near_ref.shape[0]
    copies = [
        pltpu.make_async_copy(src, dst, sems.at[i])
        for i, (src, dst) in enumerate(
            [(edge_hbm, edge_counts_ref), (own_hbm.at[pl.ds(0, near)], near_ref)]
        )
    ]
    for copy in copies:
        copy.start()
    per = cap + 2
    chunks = class_ref.shape[0]
    arrived = arrived_ref[...]
    numbers = row_iota(256)
    pick = jnp.concatenate(
        [one_hot_rows(numbers[: 2 * bricks], class_ref[c : c + 1, :], 0) for c in range(chunks)], axis=1
    )
    coded = dot(pick, arrived)
    low, high = coded[:bricks], coded[bricks:]
    begin = lax.broadcasted_iota(jnp.int32, (bricks, LANES), 0) * per
    lane = lax.broadcasted_iota(jnp.int32, (bricks, LANES), 1)
    stays = lane >= begin % LANES
    spread = jnp.concatenate(
        [
            jnp.concatenate([jnp.where(stays, x, 0.0), jnp.where(stays, 0.0, x)], axis=0)
            for x in (low, high)
        ],
        axis=1,
    ).astype(BF)
    chunk_id = lax.broadcasted_iota(jnp.int32, (32, 2 * bricks), 0)
    column = lax.broadcasted_iota(jnp.int32, (32, 2 * bricks), 1)
    wraps = jnp.where(column >= bricks, 1, 0)
    chunk_of = ((column - wraps * bricks) * per) // LANES + wraps
    lined = dot(jnp.where(chunk_id == chunk_of, 1.0, 0.0).astype(BF), spread)
    slot = (lined[:, :LANES] + 256.0 * lined[:, LANES:]).astype(jnp.int32) - 1
    right = jnp.concatenate([arrived, jnp.ones_like(arrived)], axis=1)
    parts = []
    for s in range(0, VOX, 256):
        table = jnp.concatenate(
            [one_hot_rows(numbers, slot[c : c + 1, :], s) for c in range(chunks)], axis=1
        )
        both = dot(table, right)
        parts.append((both[:, :LANES] / jnp.maximum(both[:, LANES:], 1.0)).astype(BF))
    voxels = jnp.concatenate(parts, axis=0)
    voxels_ref[...] = voxels
    copies[0].wait()
    edge = mix(edge_counts_ref[...], voxels, conv_ref[...]).astype(BF)
    half = first_ref.shape[0]
    odd = me_ref[0] % 2 == 1
    first_ref[...] = jnp.where(odd, edge[:half], edge[half:])
    second_ref[...] = jnp.where(odd, edge[half:], edge[:half])
    copies[1].wait()


def own_kernel(keep_ref, near_ref, own_hbm, voxels_ref, conv_ref, out_ref, far_ref, sems):
    keep, near, far = keep_ref.shape[0], near_ref.shape[0], far_ref.shape[0]
    parts = sems.shape[0]
    size = far // parts
    copies = [
        pltpu.make_async_copy(
            own_hbm.at[pl.ds(near + c * size, size)], far_ref.at[pl.ds(c * size, size)], sems.at[c]
        )
        for c in range(parts)
    ]
    for copy in copies:
        copy.start()
    width = voxels_ref.shape[1]
    starts = range(0, conv_ref.shape[0], width)
    wide = jnp.concatenate([conv_ref[s : s + width, :] for s in starts], axis=1)
    terms = lax.dot_general(
        wide, voxels_ref[...], (((0,), (1,)), ((), ())), preferred_element_type=F32
    ).astype(BF)
    side = jnp.concatenate([terms[s : s + width] for s in starts], axis=1)
    total = dot(side[:, :keep], keep_ref[...]) + dot(side[:, keep : keep + near], near_ref[...])
    for c in range(parts):
        copies[c].wait()
        begin = c * size
        at = keep + near + begin
        total += dot(side[:, at : at + size], far_ref[begin : begin + size, :])
    out_ref[...] = total.T


def final_kernel(me_ref, own_ref, voxels_ref, halo_ref, first_ref, second_ref, gain_ref, out_ref):
    numbers = row_iota(256)
    odd = me_ref[0] % 2 == 1
    first, second = first_ref[...], second_ref[...]
    lower, upper = jnp.where(odd, first, second), jnp.where(odd, second, first)
    partial = jnp.concatenate([lower, upper], axis=0)
    for s in range(0, VOX, 256):
        place = one_hot_rows(numbers, halo_ref[...], s)
        conv_sum = own_ref[s : s + 256, :] + dot(place, partial)
        inv_rms = lax.rsqrt(jnp.mean(conv_sum * conv_sum, axis=1, keepdims=True) + 1e-05)
        fresh = jnp.maximum(conv_sum * inv_rms * gain_ref[...], 0.0)
        out_ref[s : s + 256, :] = (voxels_ref[s : s + 256, :].astype(F32) + fresh).astype(BF)


def params(mib, semantics=None):
    return pltpu.CompilerParams(vmem_limit_bytes=mib * 1024 * 1024, dimension_semantics=semantics)


def in_hbm(x):
    return pltpu.with_memory_space_constraint(x, pltpu.HBM)


def in_vmem(x):
    return pltpu.with_memory_space_constraint(x, pltpu.VMEM)


def cost(flops, moved):
    return pl.CostEstimate(flops=int(flops), bytes_accessed=int(moved), transcendentals=0)


def per_device(
    tokens, token_voxel, in_weight, conv_weight, channel_gain, rule_in, rule_out, halo_slots
):
    bricks = lax.axis_size("brick")
    tok_count = tokens.shape[0]
    cap = 2 * tok_count // bricks
    per = cap + 2
    rows = bricks * per
    offsets, width = conv_weight.shape[0], conv_weight.shape[2]
    pairs = rule_in.shape[2]
    edges = 2 * halo_slots.shape[2]
    me = lax.axis_index("brick").astype(jnp.int32).reshape(1)
    row_number = np.arange(rows)
    brick_of, rank_of = row_number // per, row_number % per
    classes = np.where(rank_of >= cap, (rank_of - cap) * bricks + brick_of, -1)
    classes = jnp.asarray(classes.reshape(rows // LANES, LANES), jnp.int32)
    conv_rows = conv_weight.reshape(offsets * width, width)
    vmem = pl.BlockSpec(memory_space=pltpu.VMEM)
    hbm = pl.BlockSpec(memory_space=pl.ANY)
    smem = pl.BlockSpec(memory_space=pltpu.SMEM)

    send = pl.pallas_call(
        functools.partial(prep_kernel, bricks, cap),
        out_shape=pltpu.HBM((rows, width), BF),
        in_specs=[smem] + [hbm] * 3,
        out_specs=hbm,
        scratch_shapes=[
            pltpu.VMEM((tok_count // LANES, LANES), jnp.int32),
            pltpu.VMEM(tokens.shape, BF),
            pltpu.VMEM(in_weight.shape, BF),
            pltpu.VMEM((rows, width), BF),
            pltpu.SemaphoreType.DMA((3,)),
            pltpu.SemaphoreType.DMA((-(-rows // PACK),)),
        ],
        compiler_params=params(PREP_MIB),
        cost_estimate=cost(2 * rows * 1152 * width, 2_000_000),
        name="prep",
    )(me, *[in_hbm(x) for x in (token_voxel.reshape(tok_count // LANES, LANES), tokens, in_weight)])

    arrived = lax.all_to_all(
        send.reshape(bricks, per // 2, 2, width), "brick", split_axis=0, concat_axis=0, tiled=True
    ).reshape(rows, width)

    keep_counts, own_counts, edge_counts = pl.pallas_call(
        rules_kernel,
        out_shape=(
            pltpu.VMEM((KEEP, VOX, VOX), BF),
            pltpu.HBM((offsets - KEEP, VOX, VOX), BF),
            pltpu.HBM((offsets, edges, VOX), BF),
        ),
        grid=(offsets,),
        in_specs=[pl.BlockSpec((offsets, pairs), lambda k: (0, 0))] * 2,
        out_specs=(
            pl.BlockSpec((1, VOX, VOX), lambda k: (jnp.minimum(k, KEEP - 1), 0, 0)),
            pl.BlockSpec((1, VOX, VOX), lambda k: (jnp.maximum(k - KEEP, 0), 0, 0)),
            pl.BlockSpec((1, edges, VOX), lambda k: (k, 0, 0)),
        ),
        compiler_params=params(RULES_MIB, ("arbitrary",)),
        cost_estimate=cost(2 * offsets * (VOX + edges) * VOX * pairs, 2 * offsets * (VOX + edges) * VOX),
        name="rules",
    )(rule_in[0], rule_out[0])

    own_counts = in_hbm(own_counts.reshape((offsets - KEEP) * VOX, VOX))
    edge_counts = in_hbm(edge_counts.reshape(offsets * edges, VOX))
    near = NEAR * VOX
    voxels, first, second, near_counts = pl.pallas_call(
        functools.partial(voxel_kernel, bricks, cap),
        out_shape=(
            jax.ShapeDtypeStruct((VOX, width), BF),
            jax.ShapeDtypeStruct((edges // 2, width), BF),
            jax.ShapeDtypeStruct((edges // 2, width), BF),
            pltpu.VMEM((near, VOX), BF),
        ),
        in_specs=[smem] + [vmem] * 3 + [hbm] * 2,
        out_specs=(vmem,) * 4,
        scratch_shapes=[pltpu.VMEM((offsets * edges, VOX), BF), pltpu.SemaphoreType.DMA((2,))],
        compiler_params=params(VOXEL_MIB),
        cost_estimate=cost(2 * offsets * edges * VOX * width, 6_000_000),
        name="voxel",
    )(me, arrived, classes, conv_rows, edge_counts, own_counts)

    from_first = exchanged(first, "brick", 0)
    from_second = exchanged(second, "brick", 1)

    own = pl.pallas_call(
        own_kernel,
        out_shape=jax.ShapeDtypeStruct((VOX, width), F32),
        in_specs=[vmem, vmem, hbm, vmem, vmem],
        out_specs=vmem,
        scratch_shapes=[pltpu.VMEM(((offsets - KEEP) * VOX - near, VOX), BF), pltpu.SemaphoreType.DMA((FAR_PARTS,))],
        compiler_params=params(OWN_MIB),
        cost_estimate=cost(2 * offsets * VOX * (VOX + width) * width, 2 * offsets * VOX * VOX),
        name="own",
    )(in_vmem(keep_counts.reshape(KEEP * VOX, VOX)), near_counts, own_counts, voxels, conv_rows)

    return pl.pallas_call(
        final_kernel,
        out_shape=jax.ShapeDtypeStruct((VOX, width), BF),
        in_specs=[smem] + [vmem] * 6,
        out_specs=vmem,
        compiler_params=params(FINAL_MIB),
        cost_estimate=cost(2 * VOX * width * width, 1_000_000),
        name="final",
    )(me, own, voxels, halo_slots.reshape(1, edges), from_first, from_second, channel_gain.reshape(1, width))


def solution(mesh):
    return jax.shard_map(
        per_device,
        mesh=mesh,
        in_specs=(
            P(("scene", "brick"), None),
            P(("scene", "brick")),
            P(),
            P(),
            P(),
            P(("scene", "brick"), None, None),
            P(("scene", "brick"), None, None),
            P(("scene", "brick"), None, None),
        ),
        out_specs=P(("scene", "brick"), None),
        check_vma=False,
    )
```

```python
import functools

import jax
import jax.numpy as jnp
import numpy as np
from jax import lax
from jax.experimental import pallas as pl
from jax.experimental.pallas import tpu as pltpu
from jax.sharding import PartitionSpec as P

VOX = 512
LANES = 128
BF = jnp.bfloat16
F32 = jnp.float32
PREP_MIB, RULES_MIB, VOXEL_MIB, OWN_MIB, FINAL_MIB = 16, 8, 16, 20, 4
KEEP, NEAR, FAR_PARTS, PACK = 3, 10, 4, 256


def exchanged(block, axis, first):
    pairs = [(i, i + 1) for i in range(first, lax.axis_size(axis) - 1, 2)]
    return lax.ppermute(block, axis, pairs + [(b, a) for a, b in pairs])


def dot(a, b):
    return jnp.dot(a, b, preferred_element_type=F32)


def dot_t(a, b):
    return lax.dot_general(a, b, (((1,), (1,)), ((), ())), preferred_element_type=F32)


def row_iota(rows):
    return lax.broadcasted_iota(jnp.int32, (rows, LANES), 0).astype(F32).astype(BF)


def one_hot_rows(numbers, value, start):
    rows = numbers.shape[0]
    here = jnp.clip(value - start, -1, rows).astype(F32).astype(BF)
    return jnp.where(
        numbers == jnp.broadcast_to(here, numbers.shape), jnp.ones_like(numbers), jnp.zeros_like(numbers)
    )


def prep_kernel(
    bricks, cap, me_ref, voxel_hbm, tokens_hbm, weight_hbm, out_hbm, voxel_ref, tokens_ref, weight_ref, out_ref, sems, out_sems
):
    copies = [
        pltpu.make_async_copy(src, dst, sems.at[i])
        for i, (src, dst) in enumerate(
            [(voxel_hbm, voxel_ref), (weight_hbm, weight_ref), (tokens_hbm, tokens_ref)]
        )
    ]
    for copy in copies:
        copy.start()
    copies[0].wait()
    per = cap + 2
    rows = bricks * per
    chunks = voxel_ref.shape[0]
    t_from = lax.broadcasted_iota(jnp.int32, (LANES, LANES), 0)
    t_to = lax.broadcasted_iota(jnp.int32, (LANES, LANES), 1)
    upper = jnp.where(t_from <= t_to, 1.0, 0.0).astype(BF)
    brick_id = lax.broadcasted_iota(jnp.int32, (bricks, LANES), 0)
    owners = [voxel_ref[b : b + 1, :] // VOX for b in range(chunks)]
    slots = [voxel_ref[b : b + 1, :] % VOX for b in range(chunks)]
    member = [jnp.where(brick_id == o, 1.0, 0.0) for o in owners]
    running = dot(jnp.concatenate(member, axis=0).astype(BF), upper)
    before = jnp.zeros((bricks, 1), F32)
    shift = me_ref[0] * per
    lane_id = lax.broadcasted_iota(jnp.int32, (LANES, LANES), 0)
    position, slot_cols = [], []
    for b in range(chunks):
        run = running[b * bricks : (b + 1) * bricks]
        rank = jnp.sum(member[b] * (run + before), axis=0, keepdims=True).astype(jnp.int32) - 1
        before = before + run[:, LANES - 1 :]
        position.append(owners[b] * per + rank)
        at = lane_id == (rank + shift) % LANES
        plus = slots[b] + 1
        low = jnp.where(at, (plus % 256).astype(F32), 0.0)
        high = jnp.where(at, (plus // 256).astype(F32), 0.0)
        slot_cols.append(jnp.concatenate([low, high], axis=0).astype(BF))
    slot_rows = dot_t(
        jnp.concatenate(member, axis=1).astype(BF), jnp.concatenate(slot_cols, axis=1)
    ).astype(BF)
    column = lax.broadcasted_iota(jnp.int32, (1, LANES), 1)
    position.append(jnp.where(column < bricks, column * per + cap, (column - bricks) * per + cap + 1))
    copies[1].wait()
    copies[2].wait()
    projected = dot(tokens_ref[...], weight_ref[...]).astype(BF)
    source = jnp.concatenate([projected, slot_rows[:, :LANES], slot_rows[:, LANES:]], axis=0)
    sends = []
    for i, start in enumerate(range(0, rows, PACK)):
        n = min(PACK, rows - start)
        numbers = row_iota(n)
        table = jnp.concatenate([one_hot_rows(numbers, p, start) for p in position], axis=1)
        out_ref[start : start + n, :] = dot(table, source).astype(BF)
        part = pl.ds(start, n)
        sends.append(pltpu.make_async_copy(out_ref.at[part], out_hbm.at[part], out_sems.at[i]))
        sends[i].start()
    for send in sends:
        send.wait()


def rules_kernel(rule_in_ref, rule_out_ref, keep_ref, own_ref, edge_ref):
    k = pl.program_id(0)
    pairs = rule_in_ref.shape[1]
    source = rule_in_ref[pl.ds(k, 1), :]
    target = rule_out_ref[pl.ds(k, 1), :]
    numbers = row_iota(256)

    def table(value, start, n):
        return jnp.concatenate(
            [
                one_hot_rows(numbers[:n], value[:, c : c + LANES], start)
                for c in range(0, pairs, LANES)
            ],
            axis=1,
        )

    pick = jnp.concatenate([table(source, s, 256) for s in range(0, VOX, 256)], axis=0)
    place = jnp.concatenate([table(target, s, 256) for s in range(0, VOX, 256)], axis=0)
    counts = dot_t(pick, place).astype(BF)
    own_ref[0] = counts
    keep_ref[0] = counts
    edge_ref[0] = dot_t(table(target, VOX, edge_ref.shape[1]), pick).astype(BF)


def mix(counts, voxels, weights):
    width = voxels.shape[1]
    offsets = weights.shape[0] // width
    rows = counts.shape[0] // offsets
    gathered = dot(counts, voxels).astype(BF)
    side = jnp.concatenate([gathered[k * rows : (k + 1) * rows] for k in range(offsets)], axis=1)
    return dot(side, weights)


def voxel_kernel(
    bricks, cap, me_ref, arrived_ref, class_ref, conv_ref, edge_hbm, own_hbm,
    voxels_ref, first_ref, second_ref, near_ref, edge_counts_ref, sems,
):
    near = near_ref.shape[0]
    copies = [
        pltpu.make_async_copy(src, dst, sems.at[i])
        for i, (src, dst) in enumerate(
            [(edge_hbm, edge_counts_ref), (own_hbm.at[pl.ds(0, near)], near_ref)]
        )
    ]
    for copy in copies:
        copy.start()
    per = cap + 2
    chunks = class_ref.shape[0]
    arrived = arrived_ref[...]
    numbers = row_iota(256)
    pick = jnp.concatenate(
        [one_hot_rows(numbers[: 2 * bricks], class_ref[c : c + 1, :], 0) for c in range(chunks)], axis=1
    )
    coded = dot(pick, arrived)
    low, high = coded[:bricks], coded[bricks:]
    begin = lax.broadcasted_iota(jnp.int32, (bricks, LANES), 0) * per
    lane = lax.broadcasted_iota(jnp.int32, (bricks, LANES), 1)
    stays = lane >= begin % LANES
    spread = jnp.concatenate(
        [
            jnp.concatenate([jnp.where(stays, x, 0.0), jnp.where(stays, 0.0, x)], axis=0)
            for x in (low, high)
        ],
        axis=1,
    ).astype(BF)
    chunk_id = lax.broadcasted_iota(jnp.int32, (32, 2 * bricks), 0)
    column = lax.broadcasted_iota(jnp.int32, (32, 2 * bricks), 1)
    wraps = jnp.where(column >= bricks, 1, 0)
    chunk_of = ((column - wraps * bricks) * per) // LANES + wraps
    lined = dot(jnp.where(chunk_id == chunk_of, 1.0, 0.0).astype(BF), spread)
    slot = (lined[:, :LANES] + 256.0 * lined[:, LANES:]).astype(jnp.int32) - 1
    right = jnp.concatenate([arrived, jnp.ones_like(arrived)], axis=1)
    parts = []
    for s in range(0, VOX, 256):
        table = jnp.concatenate(
            [one_hot_rows(numbers, slot[c : c + 1, :], s) for c in range(chunks)], axis=1
        )
        both = dot(table, right)
        parts.append((both[:, :LANES] / jnp.maximum(both[:, LANES:], 1.0)).astype(BF))
    voxels = jnp.concatenate(parts, axis=0)
    voxels_ref[...] = voxels
    copies[0].wait()
    edge = mix(edge_counts_ref[...], voxels, conv_ref[...]).astype(BF)
    half = first_ref.shape[0]
    odd = me_ref[0] % 2 == 1
    first_ref[...] = jnp.where(odd, edge[:half], edge[half:])
    second_ref[...] = jnp.where(odd, edge[half:], edge[:half])
    copies[1].wait()


def own_kernel(keep_ref, near_ref, own_hbm, voxels_ref, conv_ref, out_ref, far_ref, sems):
    near, far = near_ref.shape[0], far_ref.shape[0]
    parts = sems.shape[0]
    size = far // parts
    copies = [
        pltpu.make_async_copy(
            own_hbm.at[pl.ds(near + c * size, size)], far_ref.at[pl.ds(c * size, size)], sems.at[c]
        )
        for c in range(parts)
    ]
    for copy in copies:
        copy.start()
    width = voxels_ref.shape[1]
    starts = range(0, conv_ref.shape[0], width)
    wide = jnp.concatenate([conv_ref[s : s + width, :] for s in starts], axis=1)
    terms = lax.dot_general(
        wide, voxels_ref[...], (((0,), (1,)), ((), ())), preferred_element_type=F32
    ).astype(BF)
    side = jnp.concatenate([terms[s : s + width] for s in starts], axis=1)
    total = dot(side[:, near + far :], keep_ref[...]) + dot(side[:, :near], near_ref[...])
    for c in range(parts):
        copies[c].wait()
        begin = c * size
        at = near + begin
        total += dot(side[:, at : at + size], far_ref[begin : begin + size, :])
    out_ref[...] = total.T


def final_kernel(me_ref, own_ref, voxels_ref, halo_ref, first_ref, second_ref, gain_ref, out_ref):
    numbers = row_iota(256)
    odd = me_ref[0] % 2 == 1
    first, second = first_ref[...], second_ref[...]
    lower, upper = jnp.where(odd, first, second), jnp.where(odd, second, first)
    partial = jnp.concatenate([lower, upper], axis=0)
    for s in range(0, VOX, 256):
        place = one_hot_rows(numbers, halo_ref[...], s)
        conv_sum = own_ref[s : s + 256, :] + dot(place, partial)
        inv_rms = lax.rsqrt(jnp.mean(conv_sum * conv_sum, axis=1, keepdims=True) + 1e-05)
        fresh = jnp.maximum(conv_sum * inv_rms * gain_ref[...], 0.0)
        out_ref[s : s + 256, :] = (voxels_ref[s : s + 256, :].astype(F32) + fresh).astype(BF)


def params(mib, semantics=None):
    return pltpu.CompilerParams(vmem_limit_bytes=mib * 1024 * 1024, dimension_semantics=semantics)


def in_hbm(x):
    return pltpu.with_memory_space_constraint(x, pltpu.HBM)


def in_vmem(x):
    return pltpu.with_memory_space_constraint(x, pltpu.VMEM)


def cost(flops, moved):
    return pl.CostEstimate(flops=int(flops), bytes_accessed=int(moved), transcendentals=0)


def per_device(
    tokens, token_voxel, in_weight, conv_weight, channel_gain, rule_in, rule_out, halo_slots
):
    bricks = lax.axis_size("brick")
    tok_count = tokens.shape[0]
    cap = 2 * tok_count // bricks
    per = cap + 2
    rows = bricks * per
    offsets, width = conv_weight.shape[0], conv_weight.shape[2]
    pairs = rule_in.shape[2]
    edges = 2 * halo_slots.shape[2]
    me = lax.axis_index("brick").astype(jnp.int32).reshape(1)
    row_number = np.arange(rows)
    brick_of, rank_of = row_number // per, row_number % per
    classes = np.where(rank_of >= cap, (rank_of - cap) * bricks + brick_of, -1)
    classes = jnp.asarray(classes.reshape(rows // LANES, LANES), jnp.int32)
    conv_rows = conv_weight.reshape(offsets * width, width)
    vmem = pl.BlockSpec(memory_space=pltpu.VMEM)
    hbm = pl.BlockSpec(memory_space=pl.ANY)
    smem = pl.BlockSpec(memory_space=pltpu.SMEM)

    send = pl.pallas_call(
        functools.partial(prep_kernel, bricks, cap),
        out_shape=pltpu.HBM((rows, width), BF),
        in_specs=[smem] + [hbm] * 3,
        out_specs=hbm,
        scratch_shapes=[
            pltpu.VMEM((tok_count // LANES, LANES), jnp.int32),
            pltpu.VMEM(tokens.shape, BF),
            pltpu.VMEM(in_weight.shape, BF),
            pltpu.VMEM((rows, width), BF),
            pltpu.SemaphoreType.DMA((3,)),
            pltpu.SemaphoreType.DMA((-(-rows // PACK),)),
        ],
        compiler_params=params(PREP_MIB),
        cost_estimate=cost(2 * rows * 1152 * width, 2_000_000),
        name="prep",
    )(me, *[in_hbm(x) for x in (token_voxel.reshape(tok_count // LANES, LANES), tokens, in_weight)])

    arrived = lax.all_to_all(
        send.reshape(bricks, per // 2, 2, width), "brick", split_axis=0, concat_axis=0, tiled=True
    ).reshape(rows, width)

    keep_counts, own_counts, edge_counts = pl.pallas_call(
        rules_kernel,
        out_shape=(
            pltpu.VMEM((KEEP, VOX, VOX), BF),
            pltpu.HBM((offsets - KEEP + 1, VOX, VOX), BF),
            pltpu.HBM((offsets, edges, VOX), BF),
        ),
        grid=(offsets,),
        in_specs=[pl.BlockSpec((offsets, pairs), lambda k: (0, 0))] * 2,
        out_specs=(
            pl.BlockSpec((1, VOX, VOX), lambda k: (jnp.maximum(k - (offsets - KEEP), 0), 0, 0)),
            pl.BlockSpec((1, VOX, VOX), lambda k: (jnp.minimum(k, offsets - KEEP), 0, 0)),
            pl.BlockSpec((1, edges, VOX), lambda k: (k, 0, 0)),
        ),
        compiler_params=params(RULES_MIB, ("arbitrary",)),
        cost_estimate=cost(2 * offsets * (VOX + edges) * VOX * pairs, 2 * offsets * (VOX + edges) * VOX),
        name="rules",
    )(rule_in[0], rule_out[0])

    own_counts = in_hbm(own_counts.reshape((offsets - KEEP + 1) * VOX, VOX))
    edge_counts = in_hbm(edge_counts.reshape(offsets * edges, VOX))
    near = NEAR * VOX
    voxels, first, second, near_counts = pl.pallas_call(
        functools.partial(voxel_kernel, bricks, cap),
        out_shape=(
            jax.ShapeDtypeStruct((VOX, width), BF),
            jax.ShapeDtypeStruct((edges // 2, width), BF),
            jax.ShapeDtypeStruct((edges // 2, width), BF),
            pltpu.VMEM((near, VOX), BF),
        ),
        in_specs=[smem] + [vmem] * 3 + [hbm] * 2,
        out_specs=(vmem,) * 4,
        scratch_shapes=[pltpu.VMEM((offsets * edges, VOX), BF), pltpu.SemaphoreType.DMA((2,))],
        compiler_params=params(VOXEL_MIB),
        cost_estimate=cost(2 * offsets * edges * VOX * width, 6_000_000),
        name="voxel",
    )(me, arrived, classes, conv_rows, edge_counts, own_counts)

    from_first = exchanged(first, "brick", 0)
    from_second = exchanged(second, "brick", 1)

    own = pl.pallas_call(
        own_kernel,
        out_shape=jax.ShapeDtypeStruct((VOX, width), F32),
        in_specs=[vmem, vmem, hbm, vmem, vmem],
        out_specs=vmem,
        scratch_shapes=[pltpu.VMEM(((offsets - KEEP) * VOX - near, VOX), BF), pltpu.SemaphoreType.DMA((FAR_PARTS,))],
        compiler_params=params(OWN_MIB),
        cost_estimate=cost(2 * offsets * VOX * (VOX + width) * width, 2 * offsets * VOX * VOX),
        name="own",
    )(in_vmem(keep_counts.reshape(KEEP * VOX, VOX)), near_counts, own_counts, voxels, conv_rows)

    return pl.pallas_call(
        final_kernel,
        out_shape=jax.ShapeDtypeStruct((VOX, width), BF),
        in_specs=[smem] + [vmem] * 6,
        out_specs=vmem,
        compiler_params=params(FINAL_MIB),
        cost_estimate=cost(2 * VOX * width * width, 1_000_000),
        name="final",
    )(me, own, voxels, halo_slots.reshape(1, edges), from_first, from_second, channel_gain.reshape(1, width))


def solution(mesh):
    return jax.shard_map(
        per_device,
        mesh=mesh,
        in_specs=(
            P(("scene", "brick"), None),
            P(("scene", "brick")),
            P(),
            P(),
            P(),
            P(("scene", "brick"), None, None),
            P(("scene", "brick"), None, None),
            P(("scene", "brick"), None, None),
        ),
        out_specs=P(("scene", "brick"), None),
        check_vma=False,
    )
```

```python
import functools

import jax
import jax.numpy as jnp
from jax import lax
from jax.experimental import pallas as pl
from jax.experimental.pallas import tpu as pltpu
from jax.sharding import PartitionSpec as P

VOX = 512
LANES = 128
BF = jnp.bfloat16
F32 = jnp.float32
PREP_MIB, RULES_MIB, VOXEL_MIB, OWN_MIB, FINAL_MIB = 16, 8, 16, 20, 4
KEEP, NEAR, FAR_PARTS, PACK = 3, 6, 6, 256


def exchanged(block, axis, first):
    pairs = [(i, i + 1) for i in range(first, lax.axis_size(axis) - 1, 2)]
    return lax.ppermute(block, axis, pairs + [(b, a) for a, b in pairs])


def dot(a, b):
    return jnp.dot(a, b, preferred_element_type=F32)


def dot_t(a, b):
    return lax.dot_general(a, b, (((1,), (1,)), ((), ())), preferred_element_type=F32)


def row_iota(rows):
    return lax.broadcasted_iota(jnp.int32, (rows, LANES), 0).astype(F32).astype(BF)


def one_hot_rows(numbers, value, start):
    rows = numbers.shape[0]
    here = jnp.clip(value - start, -1, rows).astype(F32).astype(BF)
    return jnp.where(
        numbers == jnp.broadcast_to(here, numbers.shape), jnp.ones_like(numbers), jnp.zeros_like(numbers)
    )


def prep_kernel(
    bricks, cap, me_ref, voxel_hbm, tokens_hbm, weight_hbm, out_hbm, voxel_ref, tokens_ref, weight_ref, out_ref, sems, out_sems
):
    copies = [
        pltpu.make_async_copy(src, dst, sems.at[i])
        for i, (src, dst) in enumerate(
            [(voxel_hbm, voxel_ref), (weight_hbm, weight_ref), (tokens_hbm, tokens_ref)]
        )
    ]
    for copy in copies:
        copy.start()
    copies[0].wait()
    per = cap + 2
    rows = bricks * per
    chunks = voxel_ref.shape[0]
    t_from = lax.broadcasted_iota(jnp.int32, (LANES, LANES), 0)
    t_to = lax.broadcasted_iota(jnp.int32, (LANES, LANES), 1)
    upper = jnp.where(t_from <= t_to, 1.0, 0.0).astype(BF)
    brick_id = lax.broadcasted_iota(jnp.int32, (bricks, LANES), 0)
    owners = [voxel_ref[b : b + 1, :] // VOX for b in range(chunks)]
    slots = [voxel_ref[b : b + 1, :] % VOX for b in range(chunks)]
    member = [jnp.where(brick_id == o, 1.0, 0.0) for o in owners]
    running = dot(jnp.concatenate(member, axis=0).astype(BF), upper)
    before = jnp.zeros((bricks, 1), F32)
    shift = me_ref[0] * per
    lane_id = lax.broadcasted_iota(jnp.int32, (LANES, LANES), 0)
    position, slot_cols = [], []
    for b in range(chunks):
        run = running[b * bricks : (b + 1) * bricks]
        rank = jnp.sum(member[b] * (run + before), axis=0, keepdims=True).astype(jnp.int32) - 1
        before = before + run[:, LANES - 1 :]
        position.append(owners[b] * per + rank)
        at = lane_id == (rank + shift) % LANES
        plus = slots[b] + 1
        low = jnp.where(at, (plus % 256).astype(F32), 0.0)
        high = jnp.where(at, (plus // 256).astype(F32), 0.0)
        slot_cols.append(jnp.concatenate([low, high], axis=0).astype(BF))
    slot_rows = dot_t(
        jnp.concatenate(member, axis=1).astype(BF), jnp.concatenate(slot_cols, axis=1)
    ).astype(BF)
    column = lax.broadcasted_iota(jnp.int32, (1, LANES), 1)
    position.append(jnp.where(column < bricks, column * per + cap, (column - bricks) * per + cap + 1))
    copies[1].wait()
    copies[2].wait()
    projected = dot(tokens_ref[...], weight_ref[...]).astype(BF)
    source = jnp.concatenate([projected, slot_rows[:, :LANES], slot_rows[:, LANES:]], axis=0)
    sends = []
    for i, start in enumerate(range(0, rows, PACK)):
        n = min(PACK, rows - start)
        numbers = row_iota(n)
        table = jnp.concatenate([one_hot_rows(numbers, p, start) for p in position], axis=1)
        out_ref[start : start + n, :] = dot(table, source).astype(BF)
        part = pl.ds(start, n)
        sends.append(pltpu.make_async_copy(out_ref.at[part], out_hbm.at[part], out_sems.at[i]))
        sends[i].start()
    for send in sends:
        send.wait()


def rules_kernel(rule_in_ref, rule_out_ref, keep_ref, own_ref, edge_ref):
    k = pl.program_id(0)
    pairs = rule_in_ref.shape[1]
    source = rule_in_ref[pl.ds(k, 1), :]
    target = rule_out_ref[pl.ds(k, 1), :]
    numbers = row_iota(256)

    def table(value, start, n):
        return jnp.concatenate(
            [
                one_hot_rows(numbers[:n], value[:, c : c + LANES], start)
                for c in range(0, pairs, LANES)
            ],
            axis=1,
        )

    pick = jnp.concatenate([table(source, s, 256) for s in range(0, VOX, 256)], axis=0)
    place = jnp.concatenate([table(target, s, 256) for s in range(0, VOX, 256)], axis=0)
    counts = dot_t(pick, place).astype(BF)
    own_ref[0] = counts
    keep_ref[0] = counts
    edge_ref[0] = dot_t(table(target, VOX, edge_ref.shape[1]), pick).astype(BF)


def mix(counts, voxels, weights):
    width = voxels.shape[1]
    offsets = weights.shape[0] // width
    rows = counts.shape[0] // offsets
    gathered = dot(counts, voxels).astype(BF)
    side = jnp.concatenate([gathered[k * rows : (k + 1) * rows] for k in range(offsets)], axis=1)
    return dot(side, weights)


def voxel_kernel(
    bricks, cap, me_ref, arrived_ref, conv_ref, edge_hbm, own_hbm,
    voxels_ref, first_ref, second_ref, near_ref, wide_ref, edge_counts_ref, sems,
):
    near = near_ref.shape[0]
    copies = [
        pltpu.make_async_copy(src, dst, sems.at[i])
        for i, (src, dst) in enumerate(
            [(edge_hbm, edge_counts_ref), (own_hbm.at[pl.ds(0, near)], near_ref)]
        )
    ]
    for copy in copies:
        copy.start()
    per = cap + 2
    chunks = arrived_ref.shape[0] // LANES
    arrived = arrived_ref[...]
    numbers = row_iota(256)
    wide_ref[...] = arrived.astype(F32)
    low, high = (wide_ref[pl.ds(cap + i, bricks, stride=per), :] for i in range(2))
    begin = lax.broadcasted_iota(jnp.int32, (bricks, LANES), 0) * per
    lane = lax.broadcasted_iota(jnp.int32, (bricks, LANES), 1)
    stays = lane >= begin % LANES
    spread = jnp.concatenate(
        [
            jnp.concatenate([jnp.where(stays, x, 0.0), jnp.where(stays, 0.0, x)], axis=0)
            for x in (low, high)
        ],
        axis=1,
    ).astype(BF)
    chunk_id = lax.broadcasted_iota(jnp.int32, (32, 2 * bricks), 0)
    column = lax.broadcasted_iota(jnp.int32, (32, 2 * bricks), 1)
    wraps = jnp.where(column >= bricks, 1, 0)
    chunk_of = ((column - wraps * bricks) * per) // LANES + wraps
    lined = dot(jnp.where(chunk_id == chunk_of, 1.0, 0.0).astype(BF), spread)
    slot = (lined[:, :LANES] + 256.0 * lined[:, LANES:]).astype(jnp.int32) - 1
    right = jnp.concatenate([arrived, jnp.ones_like(arrived)], axis=1)
    parts = []
    for s in range(0, VOX, 256):
        table = jnp.concatenate(
            [one_hot_rows(numbers, slot[c : c + 1, :], s) for c in range(chunks)], axis=1
        )
        both = dot(table, right)
        parts.append((both[:, :LANES] / jnp.maximum(both[:, LANES:], 1.0)).astype(BF))
    voxels = jnp.concatenate(parts, axis=0)
    voxels_ref[...] = voxels
    copies[0].wait()
    edge = mix(edge_counts_ref[...], voxels, conv_ref[...]).astype(BF)
    half = first_ref.shape[0]
    odd = me_ref[0] % 2 == 1
    first_ref[...] = jnp.where(odd, edge[:half], edge[half:])
    second_ref[...] = jnp.where(odd, edge[half:], edge[:half])
    copies[1].wait()


def own_kernel(keep_ref, near_ref, own_hbm, voxels_ref, conv_ref, out_ref, far_ref, sems):
    near, far = near_ref.shape[0], far_ref.shape[0]
    parts = sems.shape[0]
    size = far // parts
    copies = [
        pltpu.make_async_copy(
            own_hbm.at[pl.ds(near + c * size, size)], far_ref.at[pl.ds(c * size, size)], sems.at[c]
        )
        for c in range(parts)
    ]
    for copy in copies:
        copy.start()
    width = voxels_ref.shape[1]
    starts = range(0, conv_ref.shape[0], width)
    wide = jnp.concatenate([conv_ref[s : s + width, :] for s in starts], axis=1)
    terms = lax.dot_general(
        wide, voxels_ref[...], (((0,), (1,)), ((), ())), preferred_element_type=F32
    ).astype(BF)
    side = jnp.concatenate([terms[s : s + width] for s in starts], axis=1)
    total = dot(side[:, near + far :], keep_ref[...]) + dot(side[:, :near], near_ref[...])
    for c in range(parts):
        copies[c].wait()
        begin = c * size
        at = near + begin
        total += dot(side[:, at : at + size], far_ref[begin : begin + size, :])
    out_ref[...] = total.T


def final_kernel(me_ref, own_ref, voxels_ref, halo_ref, first_ref, second_ref, gain_ref, out_ref):
    numbers = row_iota(256)
    odd = me_ref[0] % 2 == 1
    first, second = first_ref[...], second_ref[...]
    lower, upper = jnp.where(odd, first, second), jnp.where(odd, second, first)
    partial = jnp.concatenate([lower, upper], axis=0)
    for s in range(0, VOX, 256):
        place = one_hot_rows(numbers, halo_ref[...], s)
        conv_sum = own_ref[s : s + 256, :] + dot(place, partial)
        inv_rms = lax.rsqrt(jnp.mean(conv_sum * conv_sum, axis=1, keepdims=True) + 1e-05)
        fresh = jnp.maximum(conv_sum * inv_rms * gain_ref[...], 0.0)
        out_ref[s : s + 256, :] = (voxels_ref[s : s + 256, :].astype(F32) + fresh).astype(BF)


def params(mib, semantics=None):
    return pltpu.CompilerParams(vmem_limit_bytes=mib * 1024 * 1024, dimension_semantics=semantics)


def in_hbm(x):
    return pltpu.with_memory_space_constraint(x, pltpu.HBM)


def in_vmem(x):
    return pltpu.with_memory_space_constraint(x, pltpu.VMEM)


def cost(flops, moved):
    return pl.CostEstimate(flops=int(flops), bytes_accessed=int(moved), transcendentals=0)


def per_device(
    tokens, token_voxel, in_weight, conv_weight, channel_gain, rule_in, rule_out, halo_slots
):
    bricks = lax.axis_size("brick")
    tok_count = tokens.shape[0]
    cap = 2 * tok_count // bricks
    per = cap + 2
    rows = bricks * per
    offsets, width = conv_weight.shape[0], conv_weight.shape[2]
    pairs = rule_in.shape[2]
    edges = 2 * halo_slots.shape[2]
    me = lax.axis_index("brick").astype(jnp.int32).reshape(1)
    conv_rows = conv_weight.reshape(offsets * width, width)
    vmem = pl.BlockSpec(memory_space=pltpu.VMEM)
    hbm = pl.BlockSpec(memory_space=pl.ANY)
    smem = pl.BlockSpec(memory_space=pltpu.SMEM)

    send = pl.pallas_call(
        functools.partial(prep_kernel, bricks, cap),
        out_shape=pltpu.HBM((rows, width), BF),
        in_specs=[smem] + [hbm] * 3,
        out_specs=hbm,
        scratch_shapes=[
            pltpu.VMEM((tok_count // LANES, LANES), jnp.int32),
            pltpu.VMEM(tokens.shape, BF),
            pltpu.VMEM(in_weight.shape, BF),
            pltpu.VMEM((rows, width), BF),
            pltpu.SemaphoreType.DMA((3,)),
            pltpu.SemaphoreType.DMA((-(-rows // PACK),)),
        ],
        compiler_params=params(PREP_MIB),
        cost_estimate=cost(2 * rows * 1152 * width, 2_000_000),
        name="prep",
    )(me, *[in_hbm(x) for x in (token_voxel.reshape(tok_count // LANES, LANES), tokens, in_weight)])

    arrived = lax.all_to_all(
        send.reshape(bricks, per // 2, 2, width), "brick", split_axis=0, concat_axis=0, tiled=True
    ).reshape(rows, width)

    keep_counts, own_counts, edge_counts = pl.pallas_call(
        rules_kernel,
        out_shape=(
            pltpu.VMEM((KEEP, VOX, VOX), BF),
            pltpu.HBM((offsets - KEEP + 1, VOX, VOX), BF),
            pltpu.HBM((offsets, edges, VOX), BF),
        ),
        grid=(offsets,),
        in_specs=[pl.BlockSpec((offsets, pairs), lambda k: (0, 0))] * 2,
        out_specs=(
            pl.BlockSpec((1, VOX, VOX), lambda k: (jnp.maximum(k - (offsets - KEEP), 0), 0, 0)),
            pl.BlockSpec((1, VOX, VOX), lambda k: (jnp.minimum(k, offsets - KEEP), 0, 0)),
            pl.BlockSpec((1, edges, VOX), lambda k: (k, 0, 0)),
        ),
        compiler_params=params(RULES_MIB, ("arbitrary",)),
        cost_estimate=cost(2 * offsets * (VOX + edges) * VOX * pairs, 2 * offsets * (VOX + edges) * VOX),
        name="rules",
    )(rule_in[0], rule_out[0])

    own_counts = in_hbm(own_counts.reshape((offsets - KEEP + 1) * VOX, VOX))
    edge_counts = in_hbm(edge_counts.reshape(offsets * edges, VOX))
    near = NEAR * VOX
    voxels, first, second, near_counts = pl.pallas_call(
        functools.partial(voxel_kernel, bricks, cap),
        out_shape=(
            jax.ShapeDtypeStruct((VOX, width), BF),
            jax.ShapeDtypeStruct((edges // 2, width), BF),
            jax.ShapeDtypeStruct((edges // 2, width), BF),
            pltpu.VMEM((near, VOX), BF),
        ),
        in_specs=[smem] + [vmem] * 2 + [hbm] * 2,
        out_specs=(vmem,) * 4,
        scratch_shapes=[
            pltpu.VMEM((rows, width), F32),
            pltpu.VMEM((offsets * edges, VOX), BF),
            pltpu.SemaphoreType.DMA((2,)),
        ],
        compiler_params=params(VOXEL_MIB),
        cost_estimate=cost(2 * offsets * edges * VOX * width, 6_000_000),
        name="voxel",
    )(me, arrived, conv_rows, edge_counts, own_counts)

    from_first = exchanged(first, "brick", 0)
    from_second = exchanged(second, "brick", 1)

    own = pl.pallas_call(
        own_kernel,
        out_shape=jax.ShapeDtypeStruct((VOX, width), F32),
        in_specs=[vmem, vmem, hbm, vmem, vmem],
        out_specs=vmem,
        scratch_shapes=[pltpu.VMEM(((offsets - KEEP) * VOX - near, VOX), BF), pltpu.SemaphoreType.DMA((FAR_PARTS,))],
        compiler_params=params(OWN_MIB),
        cost_estimate=cost(2 * offsets * VOX * (VOX + width) * width, 2 * offsets * VOX * VOX),
        name="own",
    )(in_vmem(keep_counts.reshape(KEEP * VOX, VOX)), near_counts, own_counts, voxels, conv_rows)

    return pl.pallas_call(
        final_kernel,
        out_shape=jax.ShapeDtypeStruct((VOX, width), BF),
        in_specs=[smem] + [vmem] * 6,
        out_specs=vmem,
        compiler_params=params(FINAL_MIB),
        cost_estimate=cost(2 * VOX * width * width, 1_000_000),
        name="final",
    )(me, own, voxels, halo_slots.reshape(1, edges), from_first, from_second, channel_gain.reshape(1, width))


def solution(mesh):
    return jax.shard_map(
        per_device,
        mesh=mesh,
        in_specs=(
            P(("scene", "brick"), None),
            P(("scene", "brick")),
            P(),
            P(),
            P(),
            P(("scene", "brick"), None, None),
            P(("scene", "brick"), None, None),
            P(("scene", "brick"), None, None),
        ),
        out_specs=P(("scene", "brick"), None),
        check_vma=False,
    )
```

```python
import functools

import jax
import jax.numpy as jnp
from jax import lax
from jax.experimental import pallas as pl
from jax.experimental.pallas import tpu as pltpu
from jax.sharding import PartitionSpec as P

VOX = 512
LANES = 128
BF = jnp.bfloat16
F32 = jnp.float32
PREP_MIB, RULES_MIB, VOXEL_MIB, OWN_MIB, FINAL_MIB = 16, 8, 16, 20, 4
KEEP, NEAR, FAR_PARTS, PACK = 4, 9, 4, 256


def exchanged(block, axis, first):
    pairs = [(i, i + 1) for i in range(first, lax.axis_size(axis) - 1, 2)]
    return lax.ppermute(block, axis, pairs + [(b, a) for a, b in pairs])


def dot(a, b):
    return jnp.dot(a, b, preferred_element_type=F32)


def dot_t(a, b):
    return lax.dot_general(a, b, (((1,), (1,)), ((), ())), preferred_element_type=F32)


def row_iota(rows):
    return lax.broadcasted_iota(jnp.int32, (rows, LANES), 0).astype(F32).astype(BF)


def one_hot_rows(numbers, value, start):
    rows = numbers.shape[0]
    here = jnp.clip(value - start, -1, rows).astype(F32).astype(BF)
    return jnp.where(
        numbers == jnp.broadcast_to(here, numbers.shape), jnp.ones_like(numbers), jnp.zeros_like(numbers)
    )


def prep_kernel(
    bricks, cap, me_ref, voxel_hbm, tokens_hbm, weight_hbm, out_hbm, voxel_ref, tokens_ref, weight_ref, out_ref, sems, out_sems
):
    copies = [
        pltpu.make_async_copy(src, dst, sems.at[i])
        for i, (src, dst) in enumerate(
            [(voxel_hbm, voxel_ref), (weight_hbm, weight_ref), (tokens_hbm, tokens_ref)]
        )
    ]
    for copy in copies:
        copy.start()
    copies[0].wait()
    per = cap + 2
    rows = bricks * per
    chunks = voxel_ref.shape[0]
    t_from = lax.broadcasted_iota(jnp.int32, (LANES, LANES), 0)
    t_to = lax.broadcasted_iota(jnp.int32, (LANES, LANES), 1)
    upper = jnp.where(t_from <= t_to, 1.0, 0.0).astype(BF)
    brick_id = lax.broadcasted_iota(jnp.int32, (bricks, LANES), 0)
    owners = [voxel_ref[b : b + 1, :] // VOX for b in range(chunks)]
    slots = [voxel_ref[b : b + 1, :] % VOX for b in range(chunks)]
    member = [jnp.where(brick_id == o, 1.0, 0.0) for o in owners]
    running = dot(jnp.concatenate(member, axis=0).astype(BF), upper)
    before = jnp.zeros((bricks, 1), F32)
    shift = me_ref[0] * per
    lane_id = lax.broadcasted_iota(jnp.int32, (LANES, LANES), 0)
    position, slot_cols = [], []
    for b in range(chunks):
        run = running[b * bricks : (b + 1) * bricks]
        rank = jnp.sum(member[b] * (run + before), axis=0, keepdims=True).astype(jnp.int32) - 1
        before = before + run[:, LANES - 1 :]
        position.append(owners[b] * per + rank)
        at = lane_id == (rank + shift) % LANES
        plus = slots[b] + 1
        low = jnp.where(at, (plus % 256).astype(F32), 0.0)
        high = jnp.where(at, (plus // 256).astype(F32), 0.0)
        slot_cols.append(jnp.concatenate([low, high], axis=0).astype(BF))
    slot_rows = dot_t(
        jnp.concatenate(member, axis=1).astype(BF), jnp.concatenate(slot_cols, axis=1)
    ).astype(BF)
    column = lax.broadcasted_iota(jnp.int32, (1, LANES), 1)
    position.append(jnp.where(column < bricks, column * per + cap, (column - bricks) * per + cap + 1))
    copies[1].wait()
    copies[2].wait()
    projected = dot(tokens_ref[...], weight_ref[...]).astype(BF)
    source = jnp.concatenate([projected, slot_rows[:, :LANES], slot_rows[:, LANES:]], axis=0)
    sends = []
    for i, start in enumerate(range(0, rows, PACK)):
        n = min(PACK, rows - start)
        numbers = row_iota(n)
        table = jnp.concatenate([one_hot_rows(numbers, p, start) for p in position], axis=1)
        out_ref[start : start + n, :] = dot(table, source).astype(BF)
        part = pl.ds(start, n)
        sends.append(pltpu.make_async_copy(out_ref.at[part], out_hbm.at[part], out_sems.at[i]))
        sends[i].start()
    for send in sends:
        send.wait()


def rules_kernel(rule_in_ref, rule_out_ref, keep_ref, own_ref, edge_ref):
    k = pl.program_id(0)
    pairs = rule_in_ref.shape[1]
    source = rule_in_ref[pl.ds(k, 1), :]
    target = rule_out_ref[pl.ds(k, 1), :]
    numbers = row_iota(256)

    def table(value, start, n):
        return jnp.concatenate(
            [
                one_hot_rows(numbers[:n], value[:, c : c + LANES], start)
                for c in range(0, pairs, LANES)
            ],
            axis=1,
        )

    pick = jnp.concatenate([table(source, s, 256) for s in range(0, VOX, 256)], axis=0)
    place = jnp.concatenate([table(target, s, 256) for s in range(0, VOX, 256)], axis=0)
    counts = dot_t(pick, place).astype(BF)
    own_ref[0] = counts
    keep_ref[0] = counts
    edge_ref[0] = dot_t(table(target, VOX, edge_ref.shape[1]), pick).astype(BF)


def mix(counts, voxels, weights):
    width = voxels.shape[1]
    offsets = weights.shape[0] // width
    rows = counts.shape[0] // offsets
    gathered = dot(counts, voxels).astype(BF)
    side = jnp.concatenate([gathered[k * rows : (k + 1) * rows] for k in range(offsets)], axis=1)
    return dot(side, weights)


def voxel_kernel(
    bricks, cap, me_ref, arrived_ref, conv_ref, edge_hbm, own_hbm,
    voxels_ref, first_ref, second_ref, near_ref, wide_ref, edge_counts_ref, sems,
):
    near = near_ref.shape[0]
    copies = [
        pltpu.make_async_copy(src, dst, sems.at[i])
        for i, (src, dst) in enumerate(
            [(edge_hbm, edge_counts_ref), (own_hbm.at[pl.ds(0, near)], near_ref)]
        )
    ]
    for copy in copies:
        copy.start()
    per = cap + 2
    chunks = arrived_ref.shape[0] // LANES
    arrived = arrived_ref[...]
    numbers = row_iota(256)
    wide_ref[...] = arrived.astype(F32)
    low, high = (wide_ref[pl.ds(cap + i, bricks, stride=per), :] for i in range(2))
    begin = lax.broadcasted_iota(jnp.int32, (bricks, LANES), 0) * per
    lane = lax.broadcasted_iota(jnp.int32, (bricks, LANES), 1)
    stays = lane >= begin % LANES
    spread = jnp.concatenate(
        [
            jnp.concatenate([jnp.where(stays, x, 0.0), jnp.where(stays, 0.0, x)], axis=0)
            for x in (low, high)
        ],
        axis=1,
    ).astype(BF)
    chunk_id = lax.broadcasted_iota(jnp.int32, (32, 2 * bricks), 0)
    column = lax.broadcasted_iota(jnp.int32, (32, 2 * bricks), 1)
    wraps = jnp.where(column >= bricks, 1, 0)
    chunk_of = ((column - wraps * bricks) * per) // LANES + wraps
    lined = dot(jnp.where(chunk_id == chunk_of, 1.0, 0.0).astype(BF), spread)
    slot = (lined[:, :LANES] + 256.0 * lined[:, LANES:]).astype(jnp.int32) - 1
    right = jnp.concatenate([arrived, jnp.ones_like(arrived)], axis=1)
    parts = []
    for s in range(0, VOX, 256):
        table = jnp.concatenate(
            [one_hot_rows(numbers, slot[c : c + 1, :], s) for c in range(chunks)], axis=1
        )
        both = dot(table, right)
        parts.append((both[:, :LANES] / jnp.maximum(both[:, LANES:], 1.0)).astype(BF))
    voxels = jnp.concatenate(parts, axis=0)
    voxels_ref[...] = voxels
    copies[0].wait()
    edge = mix(edge_counts_ref[...], voxels, conv_ref[...]).astype(BF)
    half = first_ref.shape[0]
    odd = me_ref[0] % 2 == 1
    first_ref[...] = jnp.where(odd, edge[:half], edge[half:])
    second_ref[...] = jnp.where(odd, edge[half:], edge[:half])
    copies[1].wait()


def own_kernel(keep_ref, near_ref, own_hbm, voxels_ref, conv_ref, out_ref, far_ref, sems):
    near, far = near_ref.shape[0], far_ref.shape[0]
    parts = sems.shape[0]
    size = far // parts
    copies = [
        pltpu.make_async_copy(
            own_hbm.at[pl.ds(near + c * size, size)], far_ref.at[pl.ds(c * size, size)], sems.at[c]
        )
        for c in range(parts)
    ]
    for copy in copies:
        copy.start()
    width = voxels_ref.shape[1]
    starts = range(0, conv_ref.shape[0], width)
    wide = jnp.concatenate([conv_ref[s : s + width, :] for s in starts], axis=1)
    terms = lax.dot_general(
        wide, voxels_ref[...], (((0,), (1,)), ((), ())), preferred_element_type=F32
    ).astype(BF)
    side = jnp.concatenate([terms[s : s + width] for s in starts], axis=1)
    total = dot(side[:, near + far :], keep_ref[...]) + dot(side[:, :near], near_ref[...])
    for c in range(parts):
        copies[c].wait()
        begin = c * size
        at = near + begin
        total += dot(side[:, at : at + size], far_ref[begin : begin + size, :])
    out_ref[...] = total.T


def final_kernel(me_ref, own_ref, voxels_ref, halo_ref, first_ref, second_ref, gain_ref, out_ref):
    numbers = row_iota(256)
    odd = me_ref[0] % 2 == 1
    first, second = first_ref[...], second_ref[...]
    lower, upper = jnp.where(odd, first, second), jnp.where(odd, second, first)
    partial = jnp.concatenate([lower, upper], axis=0)
    for s in range(0, VOX, 256):
        place = one_hot_rows(numbers, halo_ref[...], s)
        conv_sum = own_ref[s : s + 256, :] + dot(place, partial)
        inv_rms = lax.rsqrt(jnp.mean(conv_sum * conv_sum, axis=1, keepdims=True) + 1e-05)
        fresh = jnp.maximum(conv_sum * inv_rms * gain_ref[...], 0.0)
        out_ref[s : s + 256, :] = (voxels_ref[s : s + 256, :].astype(F32) + fresh).astype(BF)


def params(mib, semantics=None):
    return pltpu.CompilerParams(vmem_limit_bytes=mib * 1024 * 1024, dimension_semantics=semantics)


def in_hbm(x):
    return pltpu.with_memory_space_constraint(x, pltpu.HBM)


def in_vmem(x):
    return pltpu.with_memory_space_constraint(x, pltpu.VMEM)


def cost(flops, moved):
    return pl.CostEstimate(flops=int(flops), bytes_accessed=int(moved), transcendentals=0)


def per_device(
    tokens, token_voxel, in_weight, conv_weight, channel_gain, rule_in, rule_out, halo_slots
):
    bricks = lax.axis_size("brick")
    tok_count = tokens.shape[0]
    cap = 2 * tok_count // bricks
    per = cap + 2
    rows = bricks * per
    offsets, width = conv_weight.shape[0], conv_weight.shape[2]
    pairs = rule_in.shape[2]
    edges = 2 * halo_slots.shape[2]
    me = lax.axis_index("brick").astype(jnp.int32).reshape(1)
    conv_rows = conv_weight.reshape(offsets * width, width)
    vmem = pl.BlockSpec(memory_space=pltpu.VMEM)
    hbm = pl.BlockSpec(memory_space=pl.ANY)
    smem = pl.BlockSpec(memory_space=pltpu.SMEM)

    send = pl.pallas_call(
        functools.partial(prep_kernel, bricks, cap),
        out_shape=pltpu.HBM((rows, width), BF),
        in_specs=[smem] + [hbm] * 3,
        out_specs=hbm,
        scratch_shapes=[
            pltpu.VMEM((tok_count // LANES, LANES), jnp.int32),
            pltpu.VMEM(tokens.shape, BF),
            pltpu.VMEM(in_weight.shape, BF),
            pltpu.VMEM((rows, width), BF),
            pltpu.SemaphoreType.DMA((3,)),
            pltpu.SemaphoreType.DMA((-(-rows // PACK),)),
        ],
        compiler_params=params(PREP_MIB),
        cost_estimate=cost(2 * rows * 1152 * width, 2_000_000),
        name="prep",
    )(me, *[in_hbm(x) for x in (token_voxel.reshape(tok_count // LANES, LANES), tokens, in_weight)])

    arrived = lax.all_to_all(
        send.reshape(bricks, per // 2, 2, width), "brick", split_axis=0, concat_axis=0, tiled=True
    ).reshape(rows, width)

    keep_counts, own_counts, edge_counts = pl.pallas_call(
        rules_kernel,
        out_shape=(
            pltpu.VMEM((KEEP, VOX, VOX), BF),
            pltpu.HBM((offsets - KEEP + 1, VOX, VOX), BF),
            pltpu.HBM((offsets, edges, VOX), BF),
        ),
        grid=(offsets,),
        in_specs=[pl.BlockSpec((offsets, pairs), lambda k: (0, 0))] * 2,
        out_specs=(
            pl.BlockSpec((1, VOX, VOX), lambda k: (jnp.maximum(k - (offsets - KEEP), 0), 0, 0)),
            pl.BlockSpec((1, VOX, VOX), lambda k: (jnp.minimum(k, offsets - KEEP), 0, 0)),
            pl.BlockSpec((1, edges, VOX), lambda k: (k, 0, 0)),
        ),
        compiler_params=params(RULES_MIB, ("arbitrary",)),
        cost_estimate=cost(2 * offsets * (VOX + edges) * VOX * pairs, 2 * offsets * (VOX + edges) * VOX),
        name="rules",
    )(rule_in[0], rule_out[0])

    own_counts = in_hbm(own_counts.reshape((offsets - KEEP + 1) * VOX, VOX))
    edge_counts = in_hbm(edge_counts.reshape(offsets * edges, VOX))
    near = NEAR * VOX
    voxels, first, second, near_counts = pl.pallas_call(
        functools.partial(voxel_kernel, bricks, cap),
        out_shape=(
            jax.ShapeDtypeStruct((VOX, width), BF),
            jax.ShapeDtypeStruct((edges // 2, width), BF),
            jax.ShapeDtypeStruct((edges // 2, width), BF),
            pltpu.VMEM((near, VOX), BF),
        ),
        in_specs=[smem] + [vmem] * 2 + [hbm] * 2,
        out_specs=(vmem,) * 4,
        scratch_shapes=[
            pltpu.VMEM((rows, width), F32),
            pltpu.VMEM((offsets * edges, VOX), BF),
            pltpu.SemaphoreType.DMA((2,)),
        ],
        compiler_params=params(VOXEL_MIB),
        cost_estimate=cost(2 * offsets * edges * VOX * width, 6_000_000),
        name="voxel",
    )(me, arrived, conv_rows, edge_counts, own_counts)

    from_first = exchanged(first, "brick", 0)
    from_second = exchanged(second, "brick", 1)

    own = pl.pallas_call(
        own_kernel,
        out_shape=jax.ShapeDtypeStruct((VOX, width), F32),
        in_specs=[vmem, vmem, hbm, vmem, vmem],
        out_specs=vmem,
        scratch_shapes=[pltpu.VMEM(((offsets - KEEP) * VOX - near, VOX), BF), pltpu.SemaphoreType.DMA((FAR_PARTS,))],
        compiler_params=params(OWN_MIB),
        cost_estimate=cost(2 * offsets * VOX * (VOX + width) * width, 2 * offsets * VOX * VOX),
        name="own",
    )(in_vmem(keep_counts.reshape(KEEP * VOX, VOX)), near_counts, own_counts, voxels, conv_rows)

    return pl.pallas_call(
        final_kernel,
        out_shape=jax.ShapeDtypeStruct((VOX, width), BF),
        in_specs=[smem] + [vmem] * 6,
        out_specs=vmem,
        compiler_params=params(FINAL_MIB),
        cost_estimate=cost(2 * VOX * width * width, 1_000_000),
        name="final",
    )(me, own, voxels, halo_slots.reshape(1, edges), from_first, from_second, channel_gain.reshape(1, width))


def solution(mesh):
    return jax.shard_map(
        per_device,
        mesh=mesh,
        in_specs=(
            P(("scene", "brick"), None),
            P(("scene", "brick")),
            P(),
            P(),
            P(),
            P(("scene", "brick"), None, None),
            P(("scene", "brick"), None, None),
            P(("scene", "brick"), None, None),
        ),
        out_specs=P(("scene", "brick"), None),
        check_vma=False,
    )
```
